256 devices in a mesh: ctx: 32 (over z, x), head: 4 (over y_lo, core), rep: 2 (over y_hi).
Axes of the slice: x: 4, y: 4 (y_hi: 2, y_lo: 2; y = y_hi * 2 + y_lo), z: 8, core: 2. Of those that a mesh axis runs over, the one named last changes fastest.
Arguments:
- prefill_queries: bfloat16 [8192, 12288], P(('rep', 'ctx'), 'head'), parts along dimension 0, may hold values from -10 to 10
- prefill_keys: bfloat16 [8192, 1024], P(('rep', 'ctx'), 'head'), parts along dimension 0, may hold values from -5 to 5
- prefill_values: bfloat16 [8192, 1024], P(('rep', 'ctx'), 'head'), parts along dimension 0, may hold values from -6 to 6
- block_pair: int32 [64], P('rep'), parts along dimension 0, may hold values from 0 to 31, each once
- decode_queries: bfloat16 [64, 3, 12288], P('rep', None, 'head'), parts along dimension 0, may hold values from -10 to 10
- cache_keys: bfloat16 [64, 4096, 1024], P('rep', 'ctx', 'head'), parts along dimension 0, may hold values from -5 to 5
- cache_values: bfloat16 [64, 4096, 1024], P('rep', 'ctx', 'head'), parts along dimension 0, may hold values from -6 to 6
- draft_keys: bfloat16 [64, 3, 1024], P('rep', None, 'head'), parts along dimension 0, may hold values from -5 to 5
- draft_values: bfloat16 [64, 3, 1024], P('rep', None, 'head'), parts along dimension 0, may hold values from -6 to 6
- cache_len: int32 [64], P('rep'), parts along dimension 0, may hold values from 1 to 4096, as said below
Outputs:
- prefill_out: bfloat16 [8192, 12288], P(('rep', 'ctx'), 'head'), parts along dimension 0
- decode_out: bfloat16 [64, 3, 12288], P('rep', None, 'head'), parts along dimension 0
The draws below stay inside these ranges and needn't reach their ends.
There are 2 independent parts, one for each index of `rep`. The reference program is written for one: setup_inputs(seed, part) draws one part's arguments, and reference() takes and returns one part's arrays. A program takes and returns all parts, laid end to end along the dimension named above; each array names one. Nothing has to cross between parts.
Inputs may be any that keep to these rules, and one draw needn't show every extreme that they name: A permutation: index c of ctx holds prompt blocks block_pair[c] and 63 - block_pair[c], the lower one first. Request r holds its cache in slots 0 to cache_len[r] - 1; some request fills all 4096 slots.
All inputs are finite; a program needn't handle non-finite values.
Results may differ from the reference program's by a relative error of at most 0.004.
Values may be sent and summed in bfloat16 or wider, within the bound.
No kernel may reach another device: no remote copies, remote signals or barrier semaphores. Data moves between devices by JAX's collectives and lax.ppermute only.
A program may use at most 128 MiB of HBM per device.

```python
import jax
import jax.numpy as jnp
from jax import lax

D_HEAD = 128
HEADS = 96
KV_HEADS = 8
TOK_DEV = 128
LENGTH = 4096
ROWS = 32
CACHE = 4096
DRAFT = 3
N_CTX = 32


def loud_mix(key, base, heads_shape):
    choose = jax.random.bernoulli(jax.random.fold_in(key, 9), 0.5, heads_shape)
    flips = jax.random.bernoulli(jax.random.fold_in(key, 8), 0.5, base.shape)
    signs = jnp.where(flips, 1.0, -1.0)
    sizes = jax.random.uniform(jax.random.fold_in(key, 10), base.shape, jnp.float32, 8.0, 10.0)
    pick = jnp.repeat(choose, D_HEAD, axis=-1)
    return jnp.where(pick, signs * sizes, base)


def draw_prefill_queries(key, part):
    key = jax.random.fold_in(key, 1)
    shape = (LENGTH, HEADS * D_HEAD)
    base = jnp.clip(2.5 * jax.random.normal(key, shape, jnp.float32), -10.0, 10.0)
    return loud_mix(key, base, (LENGTH, HEADS)).astype(jnp.bfloat16)


def draw_prefill_keys(key, part):
    key = jax.random.fold_in(key, 2)
    shape = (LENGTH, KV_HEADS * D_HEAD)
    return jnp.clip(jax.random.normal(key, shape, jnp.float32), -5.0, 5.0).astype(jnp.bfloat16)


def draw_decode_queries(key, part):
    key = jax.random.fold_in(key, 3)
    shape = (ROWS, DRAFT, HEADS * D_HEAD)
    base = jnp.clip(2.5 * jax.random.normal(key, shape, jnp.float32), -10.0, 10.0)
    return loud_mix(key, base, (ROWS, DRAFT, HEADS)).astype(jnp.bfloat16)


def draw_cache_keys(key, part):
    key = jax.random.fold_in(key, 4)
    shape = (ROWS, CACHE, KV_HEADS * D_HEAD)
    return jnp.clip(jax.random.normal(key, shape, jnp.float32), -5.0, 5.0).astype(jnp.bfloat16)


def draw_draft_keys(key, part):
    key = jax.random.fold_in(key, 6)
    shape = (ROWS, DRAFT, KV_HEADS * D_HEAD)
    return jnp.clip(jax.random.normal(key, shape, jnp.float32), -5.0, 5.0).astype(jnp.bfloat16)


def draw_cache_len(key, part):
    key = jax.random.fold_in(key, 7)
    lengths = jax.random.randint(key, (ROWS,), 1, CACHE + 1)
    longest = jax.random.randint(jax.random.fold_in(key, 1), (), 0, ROWS)
    return jnp.where(jnp.arange(ROWS) == longest, CACHE, lengths).astype(jnp.int32)


def levels(rng, shape, cuts, least, high):
    loudness, own = 1.0, jax.random.fold_in(rng, 6)
    for axis_at, shards_of in cuts:
        heights = jnp.exp(jax.random.uniform(jax.random.fold_in(own, axis_at), (shards_of,), jnp.float32, least / len(cuts), high / len(cuts)))
        loudness = loudness * jnp.repeat(heights, shape[axis_at] // shards_of).reshape([-1 if axis == axis_at else 1 for axis in range(len(shape))])
    return loudness


def normal_values(stream_key, extent, width, limit, pieces=(), held_as=jnp.bfloat16):
    entries = width * jax.random.normal(stream_key, extent, jnp.float32)
    if pieces:
        entries = entries * levels(stream_key, extent, pieces, -0.22, 0.18)
    return jnp.clip(entries, -limit, limit).astype(held_as)


def setup_inputs(seed: int = 0, part: int = 0) -> dict:
    arg_keys = jax.random.split(jax.random.key(seed), 11)
    part_keys = jax.random.split(jax.random.fold_in(arg_keys[10], part), 11)
    prefill_queries = draw_prefill_queries(jax.random.fold_in(jax.random.fold_in(arg_keys[10], part), 71), part)
    prefill_keys = draw_prefill_keys(jax.random.fold_in(jax.random.fold_in(arg_keys[10], part), 71), part)
    prefill_values = normal_values(part_keys[2], (LENGTH, KV_HEADS * D_HEAD), 1.0, 6.0, ((0, 32), (1, 4)))
    block_pair = jax.random.permutation(part_keys[3], N_CTX).astype(jnp.int32)
    decode_queries = draw_decode_queries(jax.random.fold_in(jax.random.fold_in(arg_keys[10], part), 71), part)
    cache_keys = draw_cache_keys(jax.random.fold_in(jax.random.fold_in(arg_keys[10], part), 71), part)
    cache_values = normal_values(part_keys[6], (ROWS, CACHE, KV_HEADS * D_HEAD), 1.0, 6.0, ((1, 32), (2, 4)))
    draft_keys = draw_draft_keys(jax.random.fold_in(jax.random.fold_in(arg_keys[10], part), 71), part)
    draft_values = normal_values(part_keys[8], (ROWS, DRAFT, KV_HEADS * D_HEAD), 1.0, 6.0, ((2, 4),))
    cache_len = draw_cache_len(jax.random.fold_in(jax.random.fold_in(arg_keys[10], part), 71), part)
    return dict(prefill_queries=prefill_queries, prefill_keys=prefill_keys, prefill_values=prefill_values, block_pair=block_pair, decode_queries=decode_queries, cache_keys=cache_keys, cache_values=cache_values, draft_keys=draft_keys, draft_values=draft_values, cache_len=cache_len)


NEG = -1e30


def layout_positions(block_pair, rows, tok_dev):
    count = block_pair.shape[0]
    device = rows // tok_dev
    within = rows % tok_dev
    half = tok_dev // 2
    table = jnp.arange(count, dtype=jnp.int32)
    pair = jnp.sum(jnp.where(device[:, None] == table[None, :], block_pair[None, :], 0), axis=1).astype(jnp.int32)
    block = jnp.where(within < half, pair, 2 * count - 1 - pair)
    return (block * half + within % half).astype(jnp.int32)


def prefill_attention(queries, keys, values, block_pair):
    length = queries.shape[0]
    group = HEADS // KV_HEADS
    scale = D_HEAD ** -0.5
    positions = layout_positions(block_pair, jnp.arange(length, dtype=jnp.int32), TOK_DEV)
    visible = positions[None, :] <= positions[:, None]
    q_heads = queries.reshape(length, HEADS, D_HEAD).transpose(1, 0, 2)
    k_heads = keys.reshape(length, KV_HEADS, D_HEAD).transpose(1, 0, 2)
    v_heads = values.reshape(length, KV_HEADS, D_HEAD).transpose(1, 0, 2)

    def one_head(head):
        query = lax.dynamic_index_in_dim(q_heads, head, 0, keepdims=False)
        key = lax.dynamic_index_in_dim(k_heads, head // group, 0, keepdims=False)
        value = lax.dynamic_index_in_dim(v_heads, head // group, 0, keepdims=False)
        scores = jnp.dot(query, key.T, preferred_element_type=jnp.float32) * scale
        scores = jnp.where(visible, scores, NEG)
        top = jnp.max(scores, axis=1, keepdims=True)
        weights = jnp.where(visible, jnp.exp(scores - top), 0.0)
        total = jnp.sum(weights, axis=1, keepdims=True)
        mixed = jnp.dot(weights.astype(jnp.bfloat16), value, preferred_element_type=jnp.float32)
        return (mixed / total).astype(jnp.bfloat16)

    outputs = lax.map(one_head, jnp.arange(HEADS, dtype=jnp.int32))
    return outputs.transpose(1, 0, 2).reshape(length, HEADS * D_HEAD)


def decode_attention(queries, cache_keys, cache_values, draft_keys, draft_values, cache_len):
    group = HEADS // KV_HEADS
    scale = D_HEAD ** -0.5
    cache = cache_keys.shape[1]
    steps = queries.shape[1]
    slots = jnp.arange(cache, dtype=jnp.int32)
    order = jnp.arange(steps, dtype=jnp.int32)
    causal = (order[None, :] <= order[:, None])[:, None, None, :]

    def one_row(items):
        query, keys, values, new_keys, new_values, length = items
        query = query.astype(jnp.float32).reshape(steps, KV_HEADS, group, D_HEAD)
        keys = keys.astype(jnp.float32).reshape(cache, KV_HEADS, D_HEAD)
        values = values.astype(jnp.float32).reshape(cache, KV_HEADS, D_HEAD)
        new_keys = new_keys.astype(jnp.float32).reshape(steps, KV_HEADS, D_HEAD)
        new_values = new_values.astype(jnp.float32).reshape(steps, KV_HEADS, D_HEAD)
        live = slots < length
        scores = jnp.einsum("tkgd,ckd->tkgc", query, keys) * scale
        scores = jnp.where(live, scores, NEG)
        new_scores = jnp.einsum("tkgd,ukd->tkgu", query, new_keys) * scale
        new_scores = jnp.where(causal, new_scores, NEG)
        top = jnp.maximum(jnp.max(scores, axis=-1, keepdims=True), jnp.max(new_scores, axis=-1, keepdims=True))
        weights = jnp.where(live, jnp.exp(scores - top), 0.0)
        new_weights = jnp.where(causal, jnp.exp(new_scores - top), 0.0)
        total = jnp.sum(weights, axis=-1) + jnp.sum(new_weights, axis=-1)
        rounded = lax.optimization_barrier(weights.astype(jnp.bfloat16))
        new_rounded = lax.optimization_barrier(new_weights.astype(jnp.bfloat16))
        mixed = jnp.einsum("tkgc,ckd->tkgd", rounded.astype(jnp.float32), values)
        mixed = mixed + jnp.einsum("tkgu,ukd->tkgd", new_rounded.astype(jnp.float32), new_values)
        return (mixed / total[..., None]).astype(jnp.bfloat16).reshape(steps, HEADS * D_HEAD)

    return lax.map(one_row, (queries, cache_keys, cache_values, draft_keys, draft_values, cache_len))


def reference(prefill_queries, prefill_keys, prefill_values, block_pair, decode_queries, cache_keys, cache_values, draft_keys, draft_values, cache_len):
    prefill_out = prefill_attention(prefill_queries, prefill_keys, prefill_values, block_pair)
    decode_out = decode_attention(decode_queries, cache_keys, cache_values, draft_keys, draft_values, cache_len)
    return (prefill_out, decode_out)
```

```python
import functools

import jax
import jax.numpy as jnp
from jax import lax
from jax.experimental import pallas as pl
from jax.experimental.pallas import tpu as pltpu
from jax.sharding import PartitionSpec as P

D = 128
HEADS = 96
KV_HEADS = 8
GROUP = HEADS // KV_HEADS
KV_LOC = 2
H_LOC = KV_LOC * GROUP
HALF = 64
NZ, NX = 8, 4
N = NZ * NX
REQ = 32
STEPS = 3
ROWS = STEPS * H_LOC
PAY = ROWS + 8
NEG = -1e30
C2 = float(D**-0.5 * 1.4426950408889634)
CHUNK = 512
VMEM_LIMIT = 40 * 1024 * 1024
RB = 4


def row_iota(shape):
    return lax.broadcasted_iota(jnp.int32, shape, 0)


def lane_iota(shape):
    return lax.broadcasted_iota(jnp.int32, shape, 1)


def dot_t(a, b):
    return lax.dot_general(a, b, (((1,), (1,)), ((), ())), preferred_element_type=jnp.float32)


def dot(a, b):
    return lax.dot_general(a, b, (((1,), (0,)), ((), ())), preferred_element_type=jnp.float32)


def to_lanes(col_bc, rows):
    diag = row_iota((rows, D)) == lane_iota((rows, D))
    return jnp.sum(jnp.where(diag, col_bc, 0.0), axis=0, keepdims=True)


def decode_kernel(ctx_ref, len_ref, q_ref, k_ref, v_ref, out_ref):
    first = ctx_ref[0] * D
    step = pl.program_id(0)
    shape = (ROWS, 2 * D)
    lane = lane_iota(shape)
    kv_of_row = (lax.rem(row_iota(shape), H_LOC) >= GROUP).astype(jnp.int32)
    kv_of_lane = (lane >= D).astype(jnp.int32)
    same = kv_of_row == kv_of_lane
    slot = jnp.where(lane >= D, lane - D, lane) + first
    sub = row_iota((8, D))
    for i in range(RB):
        length = len_ref[step * RB + i]
        k = k_ref[i]
        v = v_ref[i]
        k2 = jnp.concatenate([k[:, :D], k[:, D:]], axis=0)
        v2 = jnp.concatenate([v[:, :D], v[:, D:]], axis=0)
        s = dot_t(q_ref[i], k2) * C2
        live = same & (slot < length)
        s = jnp.where(live, s, NEG)
        top = jnp.max(s, axis=1, keepdims=True).astype(jnp.bfloat16).astype(jnp.float32)
        p = jnp.where(live, jnp.exp2(s - top), 0.0)
        total = jnp.sum(p, axis=1, keepdims=True)
        o = dot(p.astype(jnp.bfloat16), v2)
        t_hi = total.astype(jnp.bfloat16).astype(jnp.float32)
        t_lo = total - t_hi
        m_row = to_lanes(jnp.broadcast_to(top, (ROWS, D)), ROWS)
        h_row = to_lanes(jnp.broadcast_to(t_hi, (ROWS, D)), ROWS)
        l_row = to_lanes(jnp.broadcast_to(t_lo, (ROWS, D)), ROWS)
        tail = jnp.where(sub == 0, m_row, jnp.where(sub == 1, h_row, jnp.where(sub == 2, l_row, 0.0)))
        out_ref[i] = jnp.concatenate([o, tail], axis=0).astype(jnp.bfloat16)


def decode_partials(ctx, cache_len, q72, cache_k, cache_v):
    return pl.pallas_call(
        decode_kernel,
        out_shape=jax.ShapeDtypeStruct((REQ, PAY, D), jnp.bfloat16),
        grid_spec=pltpu.PrefetchScalarGridSpec(
            num_scalar_prefetch=2,
            grid=(REQ // RB,),
            in_specs=[
                pl.BlockSpec((RB, ROWS, D), lambda i, c, n: (i, 0, 0)),
                pl.BlockSpec((RB, D, 2 * D), lambda i, c, n: (i, 0, 0)),
                pl.BlockSpec((RB, D, 2 * D), lambda i, c, n: (i, 0, 0)),
            ],
            out_specs=pl.BlockSpec((RB, PAY, D), lambda i, c, n: (i, 0, 0)),
        ),
        compiler_params=pltpu.CompilerParams(vmem_limit_bytes=VMEM_LIMIT),
        cost_estimate=pl.CostEstimate(
            flops=REQ * ROWS * 256 * D * 4, bytes_accessed=6 * 2**20, transcendentals=REQ * ROWS * 256
        ),
        name="decode_partials",
    )(ctx, cache_len, q72, cache_k, cache_v)


def combine_kernel(ctx_ref, recv_ref, q_ref, dk_ref, dv_ref, out_ref):
    dk = dk_ref[0].astype(jnp.float32)
    dv = dv_ref[0].astype(jnp.float32)
    k2 = jnp.concatenate([dk[:, :D], dk[:, D:]], axis=0).astype(jnp.bfloat16)
    v2 = jnp.concatenate([dv[:, :D], dv[:, D:]], axis=0).astype(jnp.bfloat16)
    s = dot_t(q_ref[0], k2) * C2
    shape = (ROWS, 16)
    row, lane = row_iota(shape), lane_iota(shape)
    kv_of_row = (lax.rem(row, H_LOC) >= GROUP).astype(jnp.int32)
    kv_of_lane = (lane >= 8).astype(jnp.int32)
    token = jnp.where(lane >= 8, lane - 8, lane)
    time = (row >= H_LOC).astype(jnp.int32) + (row >= 2 * H_LOC).astype(jnp.int32)
    seen = (kv_of_row == kv_of_lane) & (token <= time)
    s = jnp.where(seen, s, NEG)
    d_top = jnp.max(s, axis=1, keepdims=True)
    p = jnp.where(seen, jnp.exp2(s - d_top), 0.0)
    d_total = jnp.sum(p, axis=1, keepdims=True)
    d_out = dot(p.astype(jnp.bfloat16), v2)
    d_m = to_lanes(jnp.broadcast_to(d_top, (ROWS, D)), ROWS)
    d_l = to_lanes(jnp.broadcast_to(d_total, (ROWS, D)), ROWS)

    tails = recv_ref[:, ROWS:, :].astype(jnp.float32)
    m = tails[:, 0, :]
    total = tails[:, 1, :] + tails[:, 2, :]
    top = jnp.maximum(jnp.max(m, axis=0, keepdims=True), d_m)
    w = jnp.exp2(m - top)
    w_d = jnp.exp2(d_m - top)
    whole = jnp.sum(w * total, axis=0, keepdims=True) + w_d * d_l
    inv = 1.0 / jnp.where(whole > 0.0, whole, 1.0)
    w_all = jnp.concatenate([w * inv, jnp.broadcast_to(w_d * inv, (8, D)), jnp.zeros((D - N - 8, D), jnp.float32)], axis=0)
    w_cols = jnp.transpose(w_all)[:ROWS]
    acc = d_out * w_cols[:, N : N + 1]
    for src in range(N):
        acc = acc + recv_ref[src, :ROWS, :].astype(jnp.float32) * w_cols[:, src : src + 1]
    out_ref[...] = acc.astype(jnp.bfloat16)


def combine(ctx, recv, q72, dk8, dv8):
    return pl.pallas_call(
        combine_kernel,
        out_shape=jax.ShapeDtypeStruct((ROWS, D), jnp.bfloat16),
        grid_spec=pltpu.PrefetchScalarGridSpec(
            num_scalar_prefetch=1,
            grid=(1,),
            in_specs=[
                pl.BlockSpec((N, PAY, D), lambda i, c: (0, 0, 0)),
                pl.BlockSpec((1, ROWS, D), lambda i, c: (c[0], 0, 0)),
                pl.BlockSpec((1, 8, 2 * D), lambda i, c: (c[0], 0, 0)),
                pl.BlockSpec((1, 8, 2 * D), lambda i, c: (c[0], 0, 0)),
            ],
            out_specs=pl.BlockSpec((ROWS, D), lambda i, c: (0, 0)),
        ),
        compiler_params=pltpu.CompilerParams(vmem_limit_bytes=VMEM_LIMIT),
        cost_estimate=pl.CostEstimate(flops=4 * 2**20, bytes_accessed=2**20, transcendentals=2**14),
        name="combine",
    )(ctx, recv, q72, dk8, dv8)


def flash_step(qs_ref, kv_ref, m_ref, l_ref, acc_ref, part, kv, start, limit):
    rows = GROUP * HALF
    rb = 256
    k = kv_ref[pl.ds(start, CHUNK), kv * D : (kv + 1) * D]
    v = kv_ref[pl.ds(start, CHUNK), (KV_LOC + kv) * D : (KV_LOC + kv + 1) * D]
    for r in range(0, rows, rb):
        at = pl.ds(r, rb)
        s = dot_t(qs_ref[part, kv, at, :], k)
        if limit is not None:
            pos = start + lane_iota((rb, CHUNK))
            own = limit + (row_iota((rb, CHUNK)) & (HALF - 1))
            s = jnp.where(pos <= own, s, NEG)
        m_old = m_ref[part, kv, at, :]
        m_new = jnp.maximum(m_old, jnp.max(s, axis=1, keepdims=True))
        alpha = jnp.exp2((m_old - m_new) * C2)
        base = m_new * C2
        total = jnp.zeros((rb, D), jnp.float32)
        pieces = []
        for j in range(0, CHUNK, D):
            p = jnp.exp2(s[:, j : j + D] * C2 - base)
            total = total + p
            pieces.append(p.astype(jnp.bfloat16))
        p16 = jnp.concatenate(pieces, axis=1)
        l_ref[part, kv, at, :] = l_ref[part, kv, at, :] * alpha + total
        acc_ref[part, kv, at, :] = acc_ref[part, kv, at, :] * alpha + dot(p16, v)
        m_ref[part, kv, at, :] = m_new


def prefill_kernel(pair_ref, ctx_ref, *refs, blocks):
    n_in = len(blocks)
    q_ref = refs[0]
    srcs = refs[1 : 1 + n_in]
    out_ref = refs[1 + n_in]
    kv_lo, kv_hi, qs, m_ref, l_ref, acc_ref, sems = refs[2 + n_in :]
    ctx = ctx_ref[0]
    z, x = ctx // NX, lax.rem(ctx, NX)

    def copies():
        made = []
        for ref, (high, places) in zip(srcs, blocks):
            for j, (dz, dx) in enumerate(places):
                src = lax.rem(z + NZ - dz, NZ) * NX + lax.rem(x + NX - dx, NX)
                pair = pair_ref[src]
                if high:
                    dst = kv_hi.at[pl.ds(pl.multiple_of((N - 1 - pair) * HALF, HALF), HALF)]
                else:
                    dst = kv_lo.at[pl.ds(pl.multiple_of(pair * HALF, HALF), HALF)]
                made.append(pltpu.make_async_copy(ref.at[j], dst, sems.at[len(made)]))
        return made

    made = copies()
    for c in made:
        c.start()
    for part in range(2):
        for h in range(H_LOC):
            kv, g = divmod(h, GROUP)
            qs[part, kv, g * HALF : (g + 1) * HALF, :] = q_ref[part * HALF : (part + 1) * HALF, h * D : (h + 1) * D]
    m_ref[...] = jnp.full_like(m_ref, NEG)
    l_ref[...] = jnp.zeros_like(l_ref)
    acc_ref[...] = jnp.zeros_like(acc_ref)
    for c in made:
        c.wait()

    b = pair_ref[ctx]
    per = CHUNK // HALF
    step = functools.partial(flash_step, qs)

    def dense(ref, part, count):
        @pl.loop(0, count)
        def _(i):
            for kv in range(KV_LOC):
                step(ref, m_ref, l_ref, acc_ref, part, kv, pl.multiple_of(i * CHUNK, CHUNK), None)

    def last(ref, part, full, block):
        for kv in range(KV_LOC):
            step(ref, m_ref, l_ref, acc_ref, part, kv, pl.multiple_of(full * CHUNK, CHUNK), block * HALF)

    dense(kv_lo, 1, N * HALF // CHUNK)
    dense(kv_lo, 0, b // per)
    last(kv_lo, 0, b // per, b)
    hb = N - 1 - b
    dense(kv_hi, 1, hb // per)
    last(kv_hi, 1, hb // per, hb)
    for part in range(2):
        for h in range(H_LOC):
            kv, g = divmod(h, GROUP)
            at = pl.ds(g * HALF, HALF)
            total = jnp.sum(l_ref[part, kv, at, :], axis=1, keepdims=True)
            out_ref[part * HALF : (part + 1) * HALF, h * D : (h + 1) * D] = (acc_ref[part, kv, at, :] / total).astype(
                jnp.bfloat16
            )


def prefill(block_pair, ctx, queries, arrays, blocks):
    rows = GROUP * HALF
    return pl.pallas_call(
        functools.partial(prefill_kernel, blocks=blocks),
        out_shape=jax.ShapeDtypeStruct(queries.shape, jnp.bfloat16),
        grid_spec=pltpu.PrefetchScalarGridSpec(
            num_scalar_prefetch=2,
            grid=(1,),
            in_specs=[pl.BlockSpec(queries.shape, lambda i, p, c: (0, 0))]
            + [pl.BlockSpec(memory_space=pl.ANY)] * len(arrays),
            out_specs=pl.BlockSpec(queries.shape, lambda i, p, c: (0, 0)),
            scratch_shapes=[
                pltpu.VMEM((N * HALF, 2 * KV_LOC * D), jnp.bfloat16),
                pltpu.VMEM((N * HALF, 2 * KV_LOC * D), jnp.bfloat16),
                pltpu.VMEM((2, KV_LOC, rows, D), jnp.bfloat16),
                pltpu.VMEM((2, KV_LOC, rows, D), jnp.float32),
                pltpu.VMEM((2, KV_LOC, rows, D), jnp.float32),
                pltpu.VMEM((2, KV_LOC, rows, D), jnp.float32),
                pltpu.SemaphoreType.DMA((2 * N,)),
            ],
        ),
        compiler_params=pltpu.CompilerParams(vmem_limit_bytes=VMEM_LIMIT),
        cost_estimate=pl.CostEstimate(flops=4 * 2**30, bytes_accessed=6 * 2**20, transcendentals=7 * 2**20),
        name="prefill",
    )(block_pair, ctx, queries, *arrays)


def shift(x, dz, dx):
    def to(i):
        z, xx = divmod(i, NX)
        return ((z + dz) % NZ) * NX + (xx + dx) % NX

    return lax.ppermute(x, "ctx", [(i, to(i)) for i in range(N)])


def gather_low(own):
    parts = [own, shift(own, 0, 1), shift(own, 0, -1), shift(own, 0, 2)]
    xs = [0, 1, -1, 2]
    ring = jnp.stack(parts)
    out = [(ring, [(0, d) for d in xs])]
    up = down = ring
    for dz in range(1, 4):
        up, down = shift(up, 1, 0), shift(down, -1, 0)
        out.append((up, [(dz, d) for d in xs]))
        out.append((down, [(-dz, d) for d in xs]))
    out.append((shift(up[:2], 1, 0), [(4, d) for d in xs[:2]]))
    out.append((shift(down[2:], -1, 0), [(4, d) for d in xs[2:]]))
    return out


def gather_high(own):
    parts, zs = [own], [0]
    up = down = own
    for dz in range(1, 4):
        up, down = shift(up, 1, 0), shift(down, -1, 0)
        parts += [up, down]
        zs += [dz, -dz]
    parts.append(shift(up, 1, 0))
    zs.append(4)
    ring = jnp.stack(parts)
    right, left = shift(ring, 0, 1), shift(ring, 0, -1)
    return [
        (ring, [(d, 0) for d in zs]),
        (right, [(d, 1) for d in zs]),
        (left, [(d, -1) for d in zs]),
        (shift(right[:4], 0, 1), [(d, 2) for d in zs[:4]]),
        (shift(left[4:], 0, -1), [(d, 2) for d in zs[4:]]),
    ]


def local(
    prefill_queries,
    prefill_keys,
    prefill_values,
    block_pair,
    decode_queries,
    cache_keys,
    cache_values,
    draft_keys,
    draft_values,
    cache_len,
):
    ctx = lax.axis_index("ctx").astype(jnp.int32).reshape(1)
    kv = jnp.concatenate([prefill_keys, prefill_values], axis=1)
    low = gather_low(kv[:HALF])
    high = gather_high(kv[HALF:])

    q72 = decode_queries.reshape(REQ, ROWS, D)
    pad = ((0, 0), (0, 8 - STEPS), (0, 0))
    dk8, dv8 = jnp.pad(draft_keys, pad), jnp.pad(draft_values, pad)
    partials = decode_partials(ctx, cache_len, q72, cache_keys, cache_values)
    recv = lax.all_to_all(partials, "ctx", 0, 0, tiled=True)
    done = combine(ctx, recv, q72, dk8, dv8)
    spread = lax.all_to_all(jnp.broadcast_to(done[None], (N, ROWS, D)), "ctx", 0, 0, tiled=True)
    decode_out = spread.reshape(REQ, STEPS, H_LOC * D)

    arrays = [a for a, _ in low] + [a for a, _ in high]
    blocks = [(False, p) for _, p in low] + [(True, p) for _, p in high]
    prefill_out = prefill(block_pair, ctx, prefill_queries, arrays, blocks)
    return (prefill_out, decode_out)


def solution(mesh):
    return jax.shard_map(
        local,
        mesh=mesh,
        in_specs=(
            P(("rep", "ctx"), "head"),
            P(("rep", "ctx"), "head"),
            P(("rep", "ctx"), "head"),
            P("rep"),
            P("rep", None, "head"),
            P("rep", "ctx", "head"),
            P("rep", "ctx", "head"),
            P("rep", None, "head"),
            P("rep", None, "head"),
            P("rep"),
        ),
        out_specs=(P(("rep", "ctx"), "head"), P("rep", None, "head")),
        check_vma=False,
    )
```

```python
import functools

import jax
import jax.numpy as jnp
from jax import lax
from jax.experimental import pallas as pl
from jax.experimental.pallas import tpu as pltpu
from jax.sharding import PartitionSpec as P

D = 128
HEADS = 96
KV_HEADS = 8
GROUP = HEADS // KV_HEADS
KV_LOC = 2
H_LOC = KV_LOC * GROUP
HALF = 64
NZ, NX = 8, 4
N = NZ * NX
REQ = 32
STEPS = 3
ROWS = STEPS * H_LOC
PAY = ROWS + 8
NEG = -1e30
C2 = float(D**-0.5 * 1.4426950408889634)
CHUNK = 512
LANES = 256
QROWS = GROUP * HALF
VMEM_LIMIT = 48 * 1024 * 1024
RB = 4


def row_iota(shape):
    return lax.broadcasted_iota(jnp.int32, shape, 0)


def lane_iota(shape):
    return lax.broadcasted_iota(jnp.int32, shape, 1)


def dot_t(a, b):
    return lax.dot_general(a, b, (((1,), (1,)), ((), ())), preferred_element_type=jnp.float32)


def dot(a, b):
    return lax.dot_general(a, b, (((1,), (0,)), ((), ())), preferred_element_type=jnp.float32)


def dot_tl(a, b):
    return lax.dot_general(a, b, (((0,), (0,)), ((), ())), preferred_element_type=jnp.float32)


def to_lanes(col_bc, rows):
    diag = row_iota((rows, D)) == lane_iota((rows, D))
    return jnp.sum(jnp.where(diag, col_bc, 0.0), axis=0, keepdims=True)


def split(x, terms):
    out = []
    for _ in range(terms):
        out.append(x.astype(jnp.bfloat16).astype(jnp.float32))
        x = x - out[-1]
    return out


def decode_kernel(ctx_ref, len_ref, q_ref, k_ref, v_ref, out_ref):
    first = ctx_ref[0] * D
    step = pl.program_id(0)
    shape = (ROWS, 2 * D)
    lane = lane_iota(shape)
    kv_of_row = (lax.rem(row_iota(shape), H_LOC) >= GROUP).astype(jnp.int32)
    kv_of_lane = (lane >= D).astype(jnp.int32)
    same = kv_of_row == kv_of_lane
    slot = jnp.where(lane >= D, lane - D, lane) + first
    sub = row_iota((8, D))
    for i in range(RB):
        length = len_ref[step * RB + i]
        k = k_ref[i]
        v = v_ref[i]
        k2 = jnp.concatenate([k[:, :D], k[:, D:]], axis=0)
        v2 = jnp.concatenate([v[:, :D], v[:, D:]], axis=0)
        s = dot_t(q_ref[i], k2) * C2
        live = same & (slot < length)
        s = jnp.where(live, s, NEG)
        top = jnp.max(s, axis=1, keepdims=True)
        p = jnp.where(live, jnp.exp2(s - top), 0.0)
        total = jnp.sum(p, axis=1, keepdims=True)
        o = dot(p.astype(jnp.bfloat16), v2)
        tail = jnp.zeros((8, D), jnp.float32)
        for j, term in enumerate(split(top, 3) + split(total, 2)):
            tail = jnp.where(sub == j, to_lanes(jnp.broadcast_to(term, (ROWS, D)), ROWS), tail)
        out_ref[i] = jnp.concatenate([o, tail], axis=0).astype(jnp.bfloat16)


def decode_partials(ctx, cache_len, q72, cache_k, cache_v):
    return pl.pallas_call(
        decode_kernel,
        out_shape=jax.ShapeDtypeStruct((REQ, PAY, D), jnp.bfloat16),
        grid_spec=pltpu.PrefetchScalarGridSpec(
            num_scalar_prefetch=2,
            grid=(REQ // RB,),
            in_specs=[
                pl.BlockSpec((RB, ROWS, D), lambda i, c, n: (i, 0, 0)),
                pl.BlockSpec((RB, D, 2 * D), lambda i, c, n: (i, 0, 0)),
                pl.BlockSpec((RB, D, 2 * D), lambda i, c, n: (i, 0, 0)),
            ],
            out_specs=pl.BlockSpec((RB, PAY, D), lambda i, c, n: (i, 0, 0)),
        ),
        compiler_params=pltpu.CompilerParams(vmem_limit_bytes=VMEM_LIMIT),
        cost_estimate=pl.CostEstimate(
            flops=REQ * ROWS * 256 * D * 4, bytes_accessed=6 * 2**20, transcendentals=REQ * ROWS * 256
        ),
        name="decode_partials",
    )(ctx, cache_len, q72, cache_k, cache_v)


def combine_kernel(ctx_ref, recv_ref, q_ref, dk_ref, dv_ref, out_ref):
    dk = dk_ref[0].astype(jnp.float32)
    dv = dv_ref[0].astype(jnp.float32)
    k2 = jnp.concatenate([dk[:, :D], dk[:, D:]], axis=0).astype(jnp.bfloat16)
    v2 = jnp.concatenate([dv[:, :D], dv[:, D:]], axis=0).astype(jnp.bfloat16)
    s = dot_t(q_ref[0], k2) * C2
    shape = (ROWS, 16)
    row, lane = row_iota(shape), lane_iota(shape)
    kv_of_row = (lax.rem(row, H_LOC) >= GROUP).astype(jnp.int32)
    kv_of_lane = (lane >= 8).astype(jnp.int32)
    token = jnp.where(lane >= 8, lane - 8, lane)
    time = (row >= H_LOC).astype(jnp.int32) + (row >= 2 * H_LOC).astype(jnp.int32)
    seen = (kv_of_row == kv_of_lane) & (token <= time)
    s = jnp.where(seen, s, NEG)
    d_top = jnp.max(s, axis=1, keepdims=True)
    p = jnp.where(seen, jnp.exp2(s - d_top), 0.0)
    d_total = jnp.sum(p, axis=1, keepdims=True)
    d_out = dot(p.astype(jnp.bfloat16), v2)
    d_m = to_lanes(jnp.broadcast_to(d_top, (ROWS, D)), ROWS)
    d_l = to_lanes(jnp.broadcast_to(d_total, (ROWS, D)), ROWS)

    tails = recv_ref[:, ROWS:, :].astype(jnp.float32)
    m = (tails[:, 0, :] + tails[:, 1, :]) + tails[:, 2, :]
    total = tails[:, 3, :] + tails[:, 4, :]
    top = jnp.maximum(jnp.max(m, axis=0, keepdims=True), d_m)
    w = jnp.exp2(m - top)
    w_d = jnp.exp2(d_m - top)
    whole = jnp.sum(w * total, axis=0, keepdims=True) + w_d * d_l
    inv = 1.0 / jnp.where(whole > 0.0, whole, 1.0)
    w_all = jnp.concatenate([w * inv, jnp.broadcast_to(w_d * inv, (8, D)), jnp.zeros((D - N - 8, D), jnp.float32)], axis=0)
    w_cols = jnp.transpose(w_all)[:ROWS]
    acc = d_out * w_cols[:, N : N + 1]
    for src in range(N):
        acc = acc + recv_ref[src, :ROWS, :].astype(jnp.float32) * w_cols[:, src : src + 1]
    out_ref[...] = acc.astype(jnp.bfloat16)


def combine(ctx, recv, q72, dk8, dv8):
    return pl.pallas_call(
        combine_kernel,
        out_shape=jax.ShapeDtypeStruct((ROWS, D), jnp.bfloat16),
        grid_spec=pltpu.PrefetchScalarGridSpec(
            num_scalar_prefetch=1,
            grid=(1,),
            in_specs=[
                pl.BlockSpec((N, PAY, D), lambda i, c: (0, 0, 0)),
                pl.BlockSpec((1, ROWS, D), lambda i, c: (c[0], 0, 0)),
                pl.BlockSpec((1, 8, 2 * D), lambda i, c: (c[0], 0, 0)),
                pl.BlockSpec((1, 8, 2 * D), lambda i, c: (c[0], 0, 0)),
            ],
            out_specs=pl.BlockSpec((ROWS, D), lambda i, c: (0, 0)),
        ),
        compiler_params=pltpu.CompilerParams(vmem_limit_bytes=VMEM_LIMIT),
        cost_estimate=pl.CostEstimate(flops=4 * 2**20, bytes_accessed=2**20, transcendentals=2**14),
        name="combine",
    )(ctx, recv, q72, dk8, dv8)


def prefill_kernel(pair_ref, ctx_ref, *refs, blocks, first, final):
    refs = list(refs)
    q_ref = refs.pop(0)
    srcs = [refs.pop(0) for _ in blocks]
    if not first:
        acc_in, ml_in = refs.pop(0), refs.pop(0)
    if final:
        out_ref = refs.pop(0)
    else:
        acc_out, ml_out = refs.pop(0), refs.pop(0)
    kv_lo, kv_hi, qs, m_ref, l_ref, acc_ref, sems = refs
    ctx = ctx_ref[0]
    z, x = ctx // NX, lax.rem(ctx, NX)
    b = pair_ref[ctx]

    places = [(ref, j, dz, dx) for ref, at in zip(srcs, blocks) for j, (dz, dx) in enumerate(at)]
    n = len(places)
    pairs = [pair_ref[lax.rem(z + NZ - dz, NZ) * NX + lax.rem(x + NX - dx, NX)] for _, _, dz, dx in places]
    made = []
    n_lo = n_hi = jnp.int32(0)
    for i, (ref, j, _, _) in enumerate(places):
        rank = jnp.int32(0)
        for k in range(n):
            if k != i:
                rank = rank + (pairs[k] < pairs[i]).astype(jnp.int32)
        n_lo = n_lo + (pairs[i] < b).astype(jnp.int32)
        n_hi = n_hi + (pairs[i] > b).astype(jnp.int32)
        for half, dst, r in ((0, kv_lo, rank), (1, kv_hi, n - 1 - rank)):
            copy = pltpu.make_async_copy(
                ref.at[j, pl.ds(half * HALF, HALF)],
                dst.at[pl.ds(pl.multiple_of(r * HALF, HALF), HALF)],
                sems.at[len(made)],
            )
            copy.start()
            made.append(copy)
    for part in range(2):
        for kv in range(KV_LOC):
            rows = [
                q_ref[part * HALF : (part + 1) * HALF, (kv * GROUP + g) * D : (kv * GROUP + g + 1) * D]
                for g in range(GROUP)
            ]
            t = jnp.transpose(jnp.concatenate(rows, axis=0).astype(jnp.float32) * C2)
            top = t.astype(jnp.bfloat16)
            qs[part, kv, :D, :] = top
            qs[part, kv, D:, :] = (t - top.astype(jnp.float32)).astype(jnp.bfloat16)
    if first:
        m_ref[...] = jnp.full_like(m_ref, NEG)
        l_ref[...] = jnp.zeros_like(l_ref)
        acc_ref[...] = jnp.zeros_like(acc_ref)
    else:
        acc_ref[...] = acc_in[...]
        m_ref[...] = ml_in[:, :, 0:1, :]
        l_ref[...] = ml_in[:, :, 1:2, :]
    for copy in made:
        copy.wait()

    def step(ref, part, start, limit, diag):
        keys, values = [], []
        for kv in range(KV_LOC):
            k = ref[pl.ds(start, CHUNK), kv * D : (kv + 1) * D]
            keys.append(jnp.concatenate([k, k], axis=1))
            values.append(ref[pl.ds(start, CHUNK), (KV_LOC + kv) * D : (KV_LOC + kv + 1) * D])

        def score(kv, r):
            s = dot(keys[kv], qs[part, kv, :, r : r + LANES])
            if limit is not None:
                pos = start + row_iota((CHUNK, LANES))
                own = limit + (lane_iota((CHUNK, LANES)) & (HALF - 1)) if diag else limit - 1
                s = jnp.where(pos <= own, s, NEG)
            return s

        def soft(kv, r, s):
            at = slice(r, r + LANES)
            old = m_ref[part, kv, :, at]
            new = jnp.maximum(old, jnp.max(s, axis=0, keepdims=True))
            alpha = jnp.exp2(old - new)
            p = jnp.exp2(s - new)
            m_ref[part, kv, :, at] = new
            l_ref[part, kv, :, at] = l_ref[part, kv, :, at] * alpha + jnp.sum(p, axis=0, keepdims=True)
            return alpha, p.astype(jnp.bfloat16)

        def mix(kv, r, alpha, p):
            at = slice(r, r + LANES)
            acc_ref[part, kv, :, at] = acc_ref[part, kv, :, at] * alpha + dot_tl(values[kv], p)

        units = [(kv, r) for kv in range(KV_LOC) for r in range(0, QROWS, LANES)]
        s = score(*units[0])
        pending = None
        for i, u in enumerate(units):
            following = score(*units[i + 1]) if i + 1 < len(units) else None
            if pending is not None:
                mix(*pending)
            pending = (*u, *soft(*u, s))
            s = following
        mix(*pending)

    def dense(ref, part, count):
        @pl.loop(0, count)
        def _(i):
            step(ref, part, pl.multiple_of(i * CHUNK, CHUNK), None, False)

    def prefix(ref, part, count):
        limit = count * HALF
        full = limit // CHUNK
        dense(ref, part, full)
        start = pl.multiple_of(full * CHUNK, CHUNK)
        if first:
            step(ref, part, start, limit, True)
        else:

            @pl.when(limit > full * CHUNK)
            def _():
                step(ref, part, start, limit, False)

    dense(kv_lo, 1, n * HALF // CHUNK)
    prefix(kv_lo, 0, n_lo)
    prefix(kv_hi, 1, n_hi)
    if final:
        for part in range(2):
            for kv in range(KV_LOC):
                o = jnp.transpose(acc_ref[part, kv] / l_ref[part, kv])
                for g in range(GROUP):
                    h = kv * GROUP + g
                    out_ref[part * HALF : (part + 1) * HALF, h * D : (h + 1) * D] = o[g * HALF : (g + 1) * HALF].astype(
                        jnp.bfloat16
                    )
    else:
        acc_out[...] = acc_ref[...]
        ml_out[:, :, 0:1, :] = m_ref[...]
        ml_out[:, :, 1:2, :] = l_ref[...]
        ml_out[:, :, 2:, :] = jnp.zeros_like(ml_out[:, :, 2:, :])


def prefill(block_pair, ctx, queries, arrays, blocks, state, final):
    n = sum(len(at) for at in blocks)
    first = state is None
    acc = jax.ShapeDtypeStruct((2, KV_LOC, D, QROWS), jnp.float32)
    ml = jax.ShapeDtypeStruct((2, KV_LOC, 8, QROWS), jnp.float32)
    vmem = pl.BlockSpec(memory_space=pltpu.VMEM)
    return pl.pallas_call(
        functools.partial(prefill_kernel, blocks=blocks, first=first, final=final),
        out_shape=jax.ShapeDtypeStruct(queries.shape, jnp.bfloat16) if final else (acc, ml),
        in_specs=[pl.BlockSpec(memory_space=pltpu.SMEM)] * 2
        + [vmem]
        + [pl.BlockSpec(memory_space=pl.ANY)] * len(arrays)
        + ([] if first else [vmem, vmem]),
        out_specs=vmem if final else (vmem, vmem),
        scratch_shapes=[pltpu.VMEM((n * HALF, 2 * KV_LOC * D), jnp.bfloat16)] * 2
        + [pltpu.VMEM((2, KV_LOC, 2 * D, QROWS), jnp.bfloat16)]
        + [pltpu.VMEM((2, KV_LOC, 1, QROWS), jnp.float32)] * 2
        + [pltpu.VMEM((2, KV_LOC, D, QROWS), jnp.float32), pltpu.SemaphoreType.DMA((2 * n,))],
        compiler_params=pltpu.CompilerParams(vmem_limit_bytes=VMEM_LIMIT),
        cost_estimate=pl.CostEstimate(
            flops=n * 2**28, bytes_accessed=4 * 2**20, transcendentals=n * 2**18
        ),
        name="prefill_end" if final else "prefill_start",
    )(block_pair, ctx, queries, *arrays, *(() if first else state))


def shift(x, dz, dx):
    def to(i):
        z, xx = divmod(i, NX)
        return ((z + dz) % NZ) * NX + (xx + dx) % NX

    return lax.ppermute(x, "ctx", [(i, to(i)) for i in range(N)])


def gather(own):
    cat = functools.partial(jnp.concatenate, axis=0)
    up1, down1 = shift(own, 1, 0), shift(own, -1, 0)
    near = cat([own, up1, down1])
    near_z = [0, 1, -1]
    right1, left1 = shift(near, 0, 1), shift(near, 0, -1)
    up2, down2 = shift(near[:2], 2, 0), shift(cat([own, down1]), -2, 0)
    up4 = shift(up2[1:], 1, 0)
    far = cat([up2, down2, up4])
    far_z = [2, 3, -2, -3, 4]
    right2, left2 = shift(far, 0, 1), shift(far, 0, -1)
    right3 = shift(cat([right1[:2], right2[:2]]), 0, 1)
    left3 = shift(cat([left1[2:], left2[2:]]), 0, -1)
    early = [
        (near, [(d, 0) for d in near_z]),
        (right1, [(d, 1) for d in near_z]),
        (left1, [(d, -1) for d in near_z]),
        (far, [(d, 0) for d in far_z]),
        (right2, [(d, 1) for d in far_z]),
        (left2, [(d, -1) for d in far_z]),
    ]
    late = [
        (right3, [(d, 2) for d in near_z[:2] + far_z[:2]]),
        (left3, [(d, 2) for d in near_z[2:] + far_z[2:]]),
    ]
    return early, late


def local(
    prefill_queries,
    prefill_keys,
    prefill_values,
    block_pair,
    decode_queries,
    cache_keys,
    cache_values,
    draft_keys,
    draft_values,
    cache_len,
):
    ctx = lax.axis_index("ctx").astype(jnp.int32).reshape(1)
    kv = jnp.concatenate([prefill_keys, prefill_values], axis=1)
    early, late = gather(kv[None])

    q72 = decode_queries.reshape(REQ, ROWS, D)
    pad = ((0, 0), (0, 8 - STEPS), (0, 0))
    dk8, dv8 = jnp.pad(draft_keys, pad), jnp.pad(draft_values, pad)
    partials = decode_partials(ctx, cache_len, q72, cache_keys, cache_values)
    recv = lax.all_to_all(partials, "ctx", 0, 0, tiled=True)
    done = combine(ctx, recv, q72, dk8, dv8)
    spread = lax.all_to_all(jnp.broadcast_to(done[None], (N, ROWS, D)), "ctx", 0, 0, tiled=True)
    decode_out = spread.reshape(REQ, STEPS, H_LOC * D)

    parts = [([a for a, _ in group], [at for _, at in group]) for group in (early, late)]
    state = prefill(block_pair, ctx, prefill_queries, *parts[0], None, False)
    prefill_out = prefill(block_pair, ctx, prefill_queries, *parts[1], state, True)
    return (prefill_out, decode_out)


def solution(mesh):
    return jax.shard_map(
        local,
        mesh=mesh,
        in_specs=(
            P(("rep", "ctx"), "head"),
            P(("rep", "ctx"), "head"),
            P(("rep", "ctx"), "head"),
            P("rep"),
            P("rep", None, "head"),
            P("rep", "ctx", "head"),
            P("rep", "ctx", "head"),
            P("rep", None, "head"),
            P("rep", None, "head"),
            P("rep"),
        ),
        out_specs=(P(("rep", "ctx"), "head"), P("rep", None, "head")),
        check_vma=False,
    )
```

```python
import functools

import jax
import jax.numpy as jnp
from jax import lax
from jax.experimental import pallas as pl
from jax.experimental.pallas import tpu as pltpu
from jax.sharding import PartitionSpec as P

D = 128
HEADS = 96
KV_HEADS = 8
GROUP = HEADS // KV_HEADS
KV_LOC = 2
H_LOC = KV_LOC * GROUP
HALF = 64
NZ, NX = 8, 4
N = NZ * NX
REQ = 32
STEPS = 3
ROWS = STEPS * H_LOC
PAY = ROWS + 8
NEG = -1e30
C2 = float(D**-0.5 * 1.4426950408889634)
CHUNK = 512
LANES = 256
QROWS = GROUP * HALF
VMEM_LIMIT = 60 * 1024 * 1024
RB = 8


def row_iota(shape):
    return lax.broadcasted_iota(jnp.int32, shape, 0)


def lane_iota(shape):
    return lax.broadcasted_iota(jnp.int32, shape, 1)


def dot_t(a, b):
    return lax.dot_general(a, b, (((1,), (1,)), ((), ())), preferred_element_type=jnp.float32)


def dot(a, b):
    return lax.dot_general(a, b, (((1,), (0,)), ((), ())), preferred_element_type=jnp.float32)


def dot_tl(a, b):
    return lax.dot_general(a, b, (((0,), (0,)), ((), ())), preferred_element_type=jnp.float32)


def to_lanes(col_bc, rows):
    diag = row_iota((rows, D)) == lane_iota((rows, D))
    return jnp.sum(jnp.where(diag, col_bc, 0.0), axis=0, keepdims=True)


def split(x, terms):
    out = []
    for _ in range(terms):
        out.append(x.astype(jnp.bfloat16).astype(jnp.float32))
        x = x - out[-1]
    return out


def decode_kernel(ctx_ref, len_ref, q_ref, k_ref, v_ref, out_ref, q72_ref):
    first = ctx_ref[0] * D
    step = pl.program_id(0)
    shape = (ROWS, 2 * D)
    lane = lane_iota(shape)
    kv_of_row = (lax.rem(row_iota(shape), H_LOC) >= GROUP).astype(jnp.int32)
    kv_of_lane = (lane >= D).astype(jnp.int32)
    same = kv_of_row == kv_of_lane
    slot = jnp.where(lane >= D, lane - D, lane) + first
    sub = row_iota((8, D))
    for t in range(STEPS):
        heads = [q_ref[t, :, h * D : (h + 1) * D].astype(jnp.float32) for h in range(H_LOC)]
        turned = jnp.transpose(jnp.stack(heads), (1, 0, 2))
        q72_ref[:, t * H_LOC : (t + 1) * H_LOC, :] = turned.astype(jnp.bfloat16)

    def score(i):
        k = k_ref[i]
        k2 = jnp.concatenate([k[:, :D], k[:, D:]], axis=0)
        return dot_t(q72_ref[i], k2) * C2

    def soft(i, s):
        live = same & (slot < len_ref[step * RB + i])
        s = jnp.where(live, s, NEG)
        top = jnp.max(s, axis=1, keepdims=True)
        p = jnp.where(live, jnp.exp2(s - top), 0.0)
        return top, jnp.sum(p, axis=1, keepdims=True), p.astype(jnp.bfloat16)

    def mix(i, top, total, p):
        v = v_ref[i]
        o = dot(p, jnp.concatenate([v[:, :D], v[:, D:]], axis=0))
        tail = jnp.zeros((8, D), jnp.float32)
        for j, term in enumerate(split(top, 3) + split(total, 2)):
            tail = jnp.where(sub == j, to_lanes(jnp.broadcast_to(term, (ROWS, D)), ROWS), tail)
        out_ref[i] = jnp.concatenate([o, tail], axis=0).astype(jnp.bfloat16)

    scores = [score(i) for i in range(RB)]
    weights = [soft(i, s) for i, s in enumerate(scores)]
    for i, w in enumerate(weights):
        mix(i, *w)


def decode_partials(ctx, cache_len, queries, cache_k, cache_v):
    return pl.pallas_call(
        decode_kernel,
        out_shape=(
            jax.ShapeDtypeStruct((REQ, PAY, D), jnp.bfloat16),
            jax.ShapeDtypeStruct((REQ, ROWS, D), jnp.bfloat16),
        ),
        grid_spec=pltpu.PrefetchScalarGridSpec(
            num_scalar_prefetch=2,
            grid=(REQ // RB,),
            in_specs=[
                pl.BlockSpec((STEPS, RB, H_LOC * D), lambda i, c, n: (0, i, 0)),
                pl.BlockSpec((RB, D, 2 * D), lambda i, c, n: (i, 0, 0)),
                pl.BlockSpec((RB, D, 2 * D), lambda i, c, n: (i, 0, 0)),
            ],
            out_specs=(
                pl.BlockSpec((RB, PAY, D), lambda i, c, n: (i, 0, 0)),
                pl.BlockSpec((RB, ROWS, D), lambda i, c, n: (i, 0, 0)),
            ),
        ),
        compiler_params=pltpu.CompilerParams(vmem_limit_bytes=VMEM_LIMIT),
        cost_estimate=pl.CostEstimate(
            flops=REQ * ROWS * 256 * D * 4, bytes_accessed=6 * 2**20, transcendentals=REQ * ROWS * 256
        ),
        name="decode_partials",
    )(ctx, cache_len, queries, cache_k, cache_v)


def combine_kernel(ctx_ref, recv_ref, q_ref, dk_ref, dv_ref, out_ref):
    dk = dk_ref[0].astype(jnp.float32)
    dv = dv_ref[0].astype(jnp.float32)
    k2 = jnp.concatenate([dk[:, :D], dk[:, D:]], axis=0).astype(jnp.bfloat16)
    v2 = jnp.concatenate([dv[:, :D], dv[:, D:]], axis=0).astype(jnp.bfloat16)
    s = dot_t(q_ref[0], k2) * C2
    shape = (ROWS, 16)
    row, lane = row_iota(shape), lane_iota(shape)
    kv_of_row = (lax.rem(row, H_LOC) >= GROUP).astype(jnp.int32)
    kv_of_lane = (lane >= 8).astype(jnp.int32)
    token = jnp.where(lane >= 8, lane - 8, lane)
    time = (row >= H_LOC).astype(jnp.int32) + (row >= 2 * H_LOC).astype(jnp.int32)
    seen = (kv_of_row == kv_of_lane) & (token <= time)
    s = jnp.where(seen, s, NEG)
    d_top = jnp.max(s, axis=1, keepdims=True)
    p = jnp.where(seen, jnp.exp2(s - d_top), 0.0)
    d_total = jnp.sum(p, axis=1, keepdims=True)
    d_out = dot(p.astype(jnp.bfloat16), v2)
    d_m = to_lanes(jnp.broadcast_to(d_top, (ROWS, D)), ROWS)
    d_l = to_lanes(jnp.broadcast_to(d_total, (ROWS, D)), ROWS)

    tails = recv_ref[:, ROWS:, :].astype(jnp.float32)
    m = (tails[:, 0, :] + tails[:, 1, :]) + tails[:, 2, :]
    total = tails[:, 3, :] + tails[:, 4, :]
    top = jnp.maximum(jnp.max(m, axis=0, keepdims=True), d_m)
    w = jnp.exp2(m - top)
    w_d = jnp.exp2(d_m - top)
    whole = jnp.sum(w * total, axis=0, keepdims=True) + w_d * d_l
    inv = 1.0 / jnp.where(whole > 0.0, whole, 1.0)
    w_all = jnp.concatenate([w * inv, jnp.broadcast_to(w_d * inv, (8, D)), jnp.zeros((D - N - 8, D), jnp.float32)], axis=0)
    w_cols = jnp.transpose(w_all)[:ROWS]
    acc = d_out * w_cols[:, N : N + 1]
    for src in range(N):
        acc = acc + recv_ref[src, :ROWS, :].astype(jnp.float32) * w_cols[:, src : src + 1]
    out = acc.astype(jnp.bfloat16)
    for dst in range(N):
        out_ref[dst] = out


def combine(ctx, recv, q72, dk8, dv8):
    return pl.pallas_call(
        combine_kernel,
        out_shape=jax.ShapeDtypeStruct((N, ROWS, D), jnp.bfloat16),
        grid_spec=pltpu.PrefetchScalarGridSpec(
            num_scalar_prefetch=1,
            grid=(1,),
            in_specs=[
                pl.BlockSpec((N, PAY, D), lambda i, c: (0, 0, 0)),
                pl.BlockSpec((1, ROWS, D), lambda i, c: (c[0], 0, 0)),
                pl.BlockSpec((1, 8, 2 * D), lambda i, c: (c[0], 0, 0)),
                pl.BlockSpec((1, 8, 2 * D), lambda i, c: (c[0], 0, 0)),
            ],
            out_specs=pl.BlockSpec((N, ROWS, D), lambda i, c: (0, 0, 0)),
        ),
        compiler_params=pltpu.CompilerParams(vmem_limit_bytes=VMEM_LIMIT),
        cost_estimate=pl.CostEstimate(flops=4 * 2**20, bytes_accessed=2**20, transcendentals=2**14),
        name="combine",
    )(ctx, recv, q72, dk8, dv8)


def prefill_kernel(pair_ref, ctx_ref, *refs, blocks, first, final):
    refs = list(refs)
    q_ref = refs.pop(0)
    srcs = [refs.pop(0) for _ in blocks]
    if not first:
        acc_in, ml_in = refs.pop(0), refs.pop(0)
    if final:
        out_ref = refs.pop(0)
    else:
        acc_out, ml_out = refs.pop(0), refs.pop(0)
    kv_lo, kv_hi, qs, m_ref, l_ref, acc_ref, q_vmem, ml_vmem, sems = refs
    q_copy = pltpu.make_async_copy(q_ref, q_vmem, sems.at[0])
    q_copy.start()
    ctx = ctx_ref[0]
    z, x = ctx // NX, lax.rem(ctx, NX)
    b = pair_ref[ctx]

    places = [(ref, j, dz, dx) for ref, at in zip(srcs, blocks) for j, (dz, dx) in enumerate(at)]
    n = len(places)
    chunk = min(CHUNK, n * HALF)
    pairs = [pair_ref[lax.rem(z + NZ - dz, NZ) * NX + lax.rem(x + NX - dx, NX)] for _, _, dz, dx in places]
    ranks, low, high = [], [], []
    n_lo = n_hi = jnp.int32(0)
    for i, (ref, j, _, _) in enumerate(places):
        rank = jnp.int32(0)
        for k in range(n):
            if k != i:
                rank = rank + (pairs[k] < pairs[i]).astype(jnp.int32)
        n_lo = n_lo + (pairs[i] < b).astype(jnp.int32)
        n_hi = n_hi + (pairs[i] > b).astype(jnp.int32)
        ranks.append(rank)
        copy = pltpu.make_async_copy(
            ref.at[j, pl.ds(0, HALF)], kv_lo.at[pl.ds(pl.multiple_of(rank * HALF, HALF), HALF)], sems.at[4 + i]
        )
        copy.start()
        low.append(copy)
    for i, (ref, j, _, _) in enumerate(places):
        rank = n - 1 - ranks[i]
        copy = pltpu.make_async_copy(
            ref.at[j, pl.ds(HALF, HALF)], kv_hi.at[pl.ds(pl.multiple_of(rank * HALF, HALF), HALF)], sems.at[4 + n + i]
        )
        copy.start()
        high.append(copy)
    if not first:
        back = [
            pltpu.make_async_copy(acc_in, acc_ref, sems.at[1]),
            pltpu.make_async_copy(ml_in, ml_vmem, sems.at[2]),
        ]
        for copy in back:
            copy.start()
    q_copy.wait()
    for part in range(2):
        for kv in range(KV_LOC):
            rows = [
                q_vmem[part * HALF : (part + 1) * HALF, (kv * GROUP + g) * D : (kv * GROUP + g + 1) * D]
                for g in range(GROUP)
            ]
            t = jnp.transpose(jnp.concatenate(rows, axis=0).astype(jnp.float32) * C2)
            top = t.astype(jnp.bfloat16)
            qs[part, kv, :D, :] = top
            qs[part, kv, D:, :] = (t - top.astype(jnp.float32)).astype(jnp.bfloat16)
    if first:
        m_ref[...] = jnp.full_like(m_ref, NEG)
        l_ref[...] = jnp.zeros_like(l_ref)
        acc_ref[...] = jnp.zeros_like(acc_ref)
    else:
        for copy in back:
            copy.wait()
        m_ref[...] = ml_vmem[:, :, 0:1, :]
        l_ref[...] = ml_vmem[:, :, 1:2, :]
    if kv_lo.shape[0] > n * HALF:
        for ref in (kv_lo, kv_hi):
            ref[n * HALF :, :] = jnp.zeros((ref.shape[0] - n * HALF, ref.shape[1]), ref.dtype)
    for copy in low:
        copy.wait()

    def step(ref, part, start, limit, diag, width=chunk):
        keys, values = [], []
        for kv in range(KV_LOC):
            k = ref[pl.ds(start, width), kv * D : (kv + 1) * D]
            keys.append(jnp.concatenate([k, k], axis=1))
            values.append(ref[pl.ds(start, width), (KV_LOC + kv) * D : (KV_LOC + kv + 1) * D])

        def score(kv, r):
            s = dot(keys[kv], qs[part, kv, :, r : r + LANES])
            if limit is not None:
                pos = start + row_iota((width, LANES))
                own = limit + (lane_iota((width, LANES)) & (HALF - 1)) if diag else limit - 1
                s = jnp.where(pos <= own, s, NEG)
            return s

        def soft(kv, r, s):
            at = slice(r, r + LANES)
            old = m_ref[part, kv, :, at]
            new = jnp.maximum(old, jnp.max(s, axis=0, keepdims=True))
            alpha = jnp.exp2(old - new)
            p = jnp.exp2(s - new)
            m_ref[part, kv, :, at] = new
            l_ref[part, kv, :, at] = l_ref[part, kv, :, at] * alpha + jnp.sum(p, axis=0, keepdims=True)
            return alpha, p.astype(jnp.bfloat16)

        def mix(kv, r, alpha, p):
            at = slice(r, r + LANES)
            acc_ref[part, kv, :, at] = acc_ref[part, kv, :, at] * alpha + dot_tl(values[kv], p)

        units = [(kv, r) for kv in range(KV_LOC) for r in range(0, QROWS, LANES)]
        s = score(*units[0])
        pending = None
        for i, u in enumerate(units):
            following = score(*units[i + 1]) if i + 1 < len(units) else None
            if pending is not None:
                mix(*pending)
            pending = (*u, *soft(*u, s))
            s = following
        mix(*pending)

    def dense(ref, part, count):
        if isinstance(count, int):
            for i in range(count):
                step(ref, part, i * chunk, None, False)
            return

        @pl.loop(0, count)
        def _(i):
            step(ref, part, pl.multiple_of(i * chunk, chunk), None, False)

    def prefix(ref, part, count):
        limit = count * HALF
        full = limit // chunk
        dense(ref, part, full)
        start = pl.multiple_of(full * chunk, chunk)
        if first:
            step(ref, part, start, limit, True)
        else:

            @pl.when(limit > full * chunk)
            def _():
                step(ref, part, start, limit, False)

    dense(kv_lo, 1, n * HALF // chunk)
    if n * HALF % chunk:
        step(kv_lo, 1, n * HALF // chunk * chunk, None, False, n * HALF % chunk)
    prefix(kv_lo, 0, n_lo)
    for copy in high:
        copy.wait()
    prefix(kv_hi, 1, n_hi)
    if final:
        for part in range(2):
            for kv in range(KV_LOC):
                o = jnp.transpose(acc_ref[part, kv] / l_ref[part, kv])
                for g in range(GROUP):
                    h = kv * GROUP + g
                    out_ref[part * HALF : (part + 1) * HALF, h * D : (h + 1) * D] = o[g * HALF : (g + 1) * HALF].astype(
                        jnp.bfloat16
                    )
    else:
        acc_copy = pltpu.make_async_copy(acc_ref, acc_out, sems.at[1])
        acc_copy.start()
        ml_vmem[:, :, 0:1, :] = m_ref[...]
        ml_vmem[:, :, 1:2, :] = l_ref[...]
        ml_vmem[:, :, 2:, :] = jnp.zeros((2, KV_LOC, 6, QROWS), jnp.float32)
        ml_copy = pltpu.make_async_copy(ml_vmem, ml_out, sems.at[2])
        ml_copy.start()
        ml_copy.wait()
        acc_copy.wait()


def prefill(block_pair, ctx, queries, arrays, blocks, state, final):
    n = sum(len(at) for at in blocks)
    first = state is None
    chunk = min(CHUNK, n * HALF)
    rows = -(-n * HALF // chunk) * chunk
    acc = jax.ShapeDtypeStruct((2, KV_LOC, D, QROWS), jnp.float32)
    ml = jax.ShapeDtypeStruct((2, KV_LOC, 8, QROWS), jnp.float32)
    anywhere = pl.BlockSpec(memory_space=pl.ANY)
    return pl.pallas_call(
        functools.partial(prefill_kernel, blocks=blocks, first=first, final=final),
        out_shape=jax.ShapeDtypeStruct(queries.shape, jnp.bfloat16) if final else (acc, ml),
        in_specs=[pl.BlockSpec(memory_space=pltpu.SMEM)] * 2
        + [anywhere] * (1 + len(arrays) + (0 if first else 2)),
        out_specs=pl.BlockSpec(memory_space=pltpu.VMEM) if final else (anywhere, anywhere),
        scratch_shapes=[pltpu.VMEM((rows, 2 * KV_LOC * D), jnp.bfloat16)] * 2
        + [pltpu.VMEM((2, KV_LOC, 2 * D, QROWS), jnp.bfloat16)]
        + [pltpu.VMEM((2, KV_LOC, 1, QROWS), jnp.float32)] * 2
        + [
            pltpu.VMEM((2, KV_LOC, D, QROWS), jnp.float32),
            pltpu.VMEM(queries.shape, jnp.bfloat16),
            pltpu.VMEM((2, KV_LOC, 8, QROWS), jnp.float32),
            pltpu.SemaphoreType.DMA((4 + 2 * n,)),
        ],
        compiler_params=pltpu.CompilerParams(vmem_limit_bytes=VMEM_LIMIT),
        cost_estimate=pl.CostEstimate(
            flops=n * 2**28, bytes_accessed=4 * 2**20, transcendentals=n * 2**18
        ),
        name="prefill_end" if final else "prefill_start",
    )(block_pair, ctx, queries, *arrays, *(() if first else state))


def shift(x, dz, dx):
    def to(i):
        z, xx = divmod(i, NX)
        return ((z + dz) % NZ) * NX + (xx + dx) % NX

    return lax.ppermute(x, "ctx", [(i, to(i)) for i in range(N)])


def cat(*arrays):
    return jnp.concatenate(arrays, axis=0)


def join_kernel(*refs, ranges):
    *srcs, dst, sems = refs
    copies, at = [], 0
    for i, (src, (lo, hi)) in enumerate(zip(srcs, ranges)):
        copies.append(pltpu.make_async_copy(src.at[pl.ds(lo, hi - lo)], dst.at[pl.ds(at, hi - lo)], sems.at[i]))
        copies[-1].start()
        at += hi - lo
    for copy in copies:
        copy.wait()


def join(*pieces):
    arrays = [a for a, _, _ in pieces]
    ranges = [(lo, hi) for _, lo, hi in pieces]
    rows = sum(hi - lo for lo, hi in ranges)
    return pl.pallas_call(
        functools.partial(join_kernel, ranges=ranges),
        out_shape=jax.ShapeDtypeStruct((rows, *arrays[0].shape[1:]), arrays[0].dtype),
        in_specs=[pl.BlockSpec(memory_space=pl.ANY)] * len(arrays),
        out_specs=pl.BlockSpec(memory_space=pltpu.VMEM),
        scratch_shapes=[pltpu.SemaphoreType.DMA((len(arrays),))],
        cost_estimate=pl.CostEstimate(flops=0, bytes_accessed=rows * 2**18, transcendentals=0),
        name="join",
    )(*arrays)


def after(x, *others):
    return lax.optimization_barrier((x, *others))[0]


def local(
    prefill_queries,
    prefill_keys,
    prefill_values,
    block_pair,
    decode_queries,
    cache_keys,
    cache_values,
    draft_keys,
    draft_values,
    cache_len,
):
    ctx = lax.axis_index("ctx").astype(jnp.int32).reshape(1)
    pad = ((0, 0), (0, 8 - STEPS), (0, 0))
    dk8, dv8 = jnp.pad(draft_keys, pad), jnp.pad(draft_values, pad)

    own = jnp.concatenate([prefill_keys, prefill_values], axis=1)[None]
    up1, down1 = shift(own, 1, 0), shift(own, -1, 0)
    near, near_z = cat(own, up1, down1), [0, 1, -1]
    right1, left1, across1 = shift(near, 0, 1), shift(near, 0, -1), shift(near, 0, 2)
    up2, down2 = shift(near[:2], 2, 0), shift(cat(own, down1), -2, 0)

    turned = jnp.transpose(decode_queries, (1, 0, 2))
    partials, q72 = decode_partials(ctx, after(cache_len, up1, down1), turned, cache_keys, cache_values)

    up4 = shift(up2[1:], 1, 0)
    recv = lax.all_to_all(after(partials, right1, left1, up2, down2, up4, across1), "ctx", 0, 0, tiled=True)
    far, far_z = join((up2, 0, 2), (down2, 0, 2), (up4, 0, 1)), [2, 3, -2, -3, 4]
    right2, left2 = shift(far, 0, 1), shift(far, 0, -1)

    def at(zs, x):
        return [(d, x) for d in zs]

    state = prefill(
        block_pair,
        ctx,
        prefill_queries,
        [near, right1, left1, across1, far],
        [at(near_z, 0), at(near_z, 1), at(near_z, -1), at(near_z, 2), at(far_z, 0)],
        None,
        False,
    )
    done = combine(after(ctx, *state, right2, left2), recv, q72, dk8, dv8)
    spread = lax.all_to_all(done, "ctx", 0, 0, tiled=True)
    decode_out = spread.reshape(REQ, STEPS, H_LOC * D)

    right3, left3 = shift(right2[:3], 0, 1), shift(left2[3:], 0, -1)
    state = prefill(
        after(block_pair, done), ctx, prefill_queries, [right2, left2], [at(far_z, 1), at(far_z, -1)], state, False
    )
    last = [at(far_z[:3], 2), at(far_z[3:], 2)]
    prefill_out = prefill(block_pair, ctx, prefill_queries, [right3, left3], last, state, True)
    return (prefill_out, decode_out)


def solution(mesh):
    return jax.shard_map(
        local,
        mesh=mesh,
        in_specs=(
            P(("rep", "ctx"), "head"),
            P(("rep", "ctx"), "head"),
            P(("rep", "ctx"), "head"),
            P("rep"),
            P("rep", None, "head"),
            P("rep", "ctx", "head"),
            P("rep", "ctx", "head"),
            P("rep", None, "head"),
            P("rep", None, "head"),
            P("rep"),
        ),
        out_specs=(P(("rep", "ctx"), "head"), P("rep", None, "head")),
        check_vma=False,
    )
```

```python
import functools

import jax
import jax.numpy as jnp
from jax import lax
from jax.experimental import pallas as pl
from jax.experimental.pallas import tpu as pltpu
from jax.sharding import PartitionSpec as P

D = 128
HEADS = 96
KV_HEADS = 8
GROUP = HEADS // KV_HEADS
KV_LOC = 2
H_LOC = KV_LOC * GROUP
HALF = 64
NZ, NX = 8, 4
N = NZ * NX
REQ = 32
STEPS = 3
ROWS = STEPS * H_LOC
PAY = ROWS + 8
NEG = -1e30
C2 = float(D**-0.5 * 1.4426950408889634)
CHUNK = 512
LANES = 256
QROWS = GROUP * HALF
VMEM_LIMIT = 60 * 1024 * 1024
RB = 8


def row_iota(shape):
    return lax.broadcasted_iota(jnp.int32, shape, 0)


def lane_iota(shape):
    return lax.broadcasted_iota(jnp.int32, shape, 1)


def dot_t(a, b):
    return lax.dot_general(a, b, (((1,), (1,)), ((), ())), preferred_element_type=jnp.float32)


def dot(a, b):
    return lax.dot_general(a, b, (((1,), (0,)), ((), ())), preferred_element_type=jnp.float32)


def dot_tl(a, b):
    return lax.dot_general(a, b, (((0,), (0,)), ((), ())), preferred_element_type=jnp.float32)


def to_lanes(col_bc, rows):
    diag = row_iota((rows, D)) == lane_iota((rows, D))
    return jnp.sum(jnp.where(diag, col_bc, 0.0), axis=0, keepdims=True)


def split(x, terms):
    out = []
    for _ in range(terms):
        out.append(x.astype(jnp.bfloat16).astype(jnp.float32))
        x = x - out[-1]
    return out


def decode_kernel(base, carried, ctx_ref, len_ref, q_ref, k_ref, v_ref, *refs):
    out_ref, q72_ref = refs[carried:]
    first = ctx_ref[0] * D
    step = base + pl.program_id(0)
    shape = (ROWS, 2 * D)
    lane = lane_iota(shape)
    kv_of_row = (lax.rem(row_iota(shape), H_LOC) >= GROUP).astype(jnp.int32)
    kv_of_lane = (lane >= D).astype(jnp.int32)
    same = kv_of_row == kv_of_lane
    slot = jnp.where(lane >= D, lane - D, lane) + first
    sub = row_iota((8, D))
    for t in range(STEPS):
        heads = [q_ref[t, :, h * D : (h + 1) * D].astype(jnp.float32) for h in range(H_LOC)]
        turned = jnp.transpose(jnp.stack(heads), (1, 0, 2))
        q72_ref[:, t * H_LOC : (t + 1) * H_LOC, :] = turned.astype(jnp.bfloat16)

    def score(i):
        k = k_ref[i]
        k2 = jnp.concatenate([k[:, :D], k[:, D:]], axis=0)
        return dot_t(q72_ref[i], k2) * C2

    def soft(i, s):
        live = same & (slot < len_ref[step * RB + i])
        s = jnp.where(live, s, NEG)
        top = jnp.max(s, axis=1, keepdims=True)
        p = jnp.where(live, jnp.exp2(s - top), 0.0)
        return top, jnp.sum(p, axis=1, keepdims=True), p.astype(jnp.bfloat16)

    def mix(i, top, total, p):
        v = v_ref[i]
        o = dot(p, jnp.concatenate([v[:, :D], v[:, D:]], axis=0))
        tail = jnp.zeros((8, D), jnp.float32)
        for j, term in enumerate(split(top, 3) + split(total, 2)):
            tail = jnp.where(sub == j, to_lanes(jnp.broadcast_to(term, (ROWS, D)), ROWS), tail)
        out_ref[i] = jnp.concatenate([o, tail], axis=0).astype(jnp.bfloat16)

    scores = [score(i) for i in range(RB)]
    weights = [soft(i, s) for i, s in enumerate(scores)]
    for i, w in enumerate(weights):
        mix(i, *w)


def decode_partials(ctx, cache_len, queries, cache_k, cache_v, before):
    steps = REQ // RB // 2
    base = 0 if before is None else steps
    before = () if before is None else before
    kernel = functools.partial(decode_kernel, base, len(before))
    return pl.pallas_call(
        kernel,
        out_shape=(
            jax.ShapeDtypeStruct((REQ, PAY, D), jnp.bfloat16),
            jax.ShapeDtypeStruct((REQ, ROWS, D), jnp.bfloat16),
        ),
        grid_spec=pltpu.PrefetchScalarGridSpec(
            num_scalar_prefetch=2,
            grid=(steps,),
            in_specs=[
                pl.BlockSpec((STEPS, RB, H_LOC * D), lambda i, c, n: (0, base + i, 0)),
                pl.BlockSpec((RB, D, 2 * D), lambda i, c, n: (base + i, 0, 0)),
                pl.BlockSpec((RB, D, 2 * D), lambda i, c, n: (base + i, 0, 0)),
            ]
            + [pl.BlockSpec(memory_space=pl.ANY)] * len(before),
            out_specs=(
                pl.BlockSpec((RB, PAY, D), lambda i, c, n: (base + i, 0, 0)),
                pl.BlockSpec((RB, ROWS, D), lambda i, c, n: (base + i, 0, 0)),
            ),
        ),
        input_output_aliases={5 + i: i for i in range(len(before))},
        compiler_params=pltpu.CompilerParams(vmem_limit_bytes=VMEM_LIMIT),
        cost_estimate=pl.CostEstimate(
            flops=REQ * ROWS * 256 * D * 2, bytes_accessed=3 * 2**20, transcendentals=REQ * ROWS * 128
        ),
        name="decode_partials",
    )(ctx, cache_len, queries, cache_k, cache_v, *before)


def combine_kernel(ctx_ref, recv_ref, q_ref, dk_ref, dv_ref, out_ref):
    dk = dk_ref[0].astype(jnp.float32)
    dv = dv_ref[0].astype(jnp.float32)
    k2 = jnp.concatenate([dk[:, :D], dk[:, D:]], axis=0).astype(jnp.bfloat16)
    v2 = jnp.concatenate([dv[:, :D], dv[:, D:]], axis=0).astype(jnp.bfloat16)
    s = dot_t(q_ref[0], k2) * C2
    shape = (ROWS, 16)
    row, lane = row_iota(shape), lane_iota(shape)
    kv_of_row = (lax.rem(row, H_LOC) >= GROUP).astype(jnp.int32)
    kv_of_lane = (lane >= 8).astype(jnp.int32)
    token = jnp.where(lane >= 8, lane - 8, lane)
    time = (row >= H_LOC).astype(jnp.int32) + (row >= 2 * H_LOC).astype(jnp.int32)
    seen = (kv_of_row == kv_of_lane) & (token <= time)
    s = jnp.where(seen, s, NEG)
    d_top = jnp.max(s, axis=1, keepdims=True)
    p = jnp.where(seen, jnp.exp2(s - d_top), 0.0)
    d_total = jnp.sum(p, axis=1, keepdims=True)
    d_out = dot(p.astype(jnp.bfloat16), v2)
    d_m = to_lanes(jnp.broadcast_to(d_top, (ROWS, D)), ROWS)
    d_l = to_lanes(jnp.broadcast_to(d_total, (ROWS, D)), ROWS)

    tails = recv_ref[:, ROWS:, :].astype(jnp.float32)
    m = (tails[:, 0, :] + tails[:, 1, :]) + tails[:, 2, :]
    total = tails[:, 3, :] + tails[:, 4, :]
    top = jnp.maximum(jnp.max(m, axis=0, keepdims=True), d_m)
    w = jnp.exp2(m - top)
    w_d = jnp.exp2(d_m - top)
    whole = jnp.sum(w * total, axis=0, keepdims=True) + w_d * d_l
    inv = 1.0 / jnp.where(whole > 0.0, whole, 1.0)
    w_all = jnp.concatenate([w * inv, jnp.broadcast_to(w_d * inv, (8, D)), jnp.zeros((D - N - 8, D), jnp.float32)], axis=0)
    w_cols = jnp.transpose(w_all)[:ROWS]
    acc = d_out * w_cols[:, N : N + 1]
    for src in range(N):
        acc = acc + recv_ref[src, :ROWS, :].astype(jnp.float32) * w_cols[:, src : src + 1]
    out = acc.astype(jnp.bfloat16)
    for dst in range(N):
        out_ref[dst] = out


def combine(ctx, recv, q72, dk8, dv8):
    return pl.pallas_call(
        combine_kernel,
        out_shape=jax.ShapeDtypeStruct((N, ROWS, D), jnp.bfloat16),
        grid_spec=pltpu.PrefetchScalarGridSpec(
            num_scalar_prefetch=1,
            grid=(1,),
            in_specs=[
                pl.BlockSpec((N, PAY, D), lambda i, c: (0, 0, 0)),
                pl.BlockSpec((1, ROWS, D), lambda i, c: (c[0], 0, 0)),
                pl.BlockSpec((1, 8, 2 * D), lambda i, c: (c[0], 0, 0)),
                pl.BlockSpec((1, 8, 2 * D), lambda i, c: (c[0], 0, 0)),
            ],
            out_specs=pl.BlockSpec((N, ROWS, D), lambda i, c: (0, 0, 0)),
        ),
        compiler_params=pltpu.CompilerParams(vmem_limit_bytes=8 * 1024 * 1024),
        cost_estimate=pl.CostEstimate(flops=4 * 2**20, bytes_accessed=2**20, transcendentals=2**14),
        name="combine",
    )(ctx, recv, q72, dk8, dv8)


def prefill_kernel(pair_ref, ctx_ref, *refs, blocks, first, final):
    refs = list(refs)
    q_ref = refs.pop(0)
    srcs = [refs.pop(0) for _ in blocks]
    if not first:
        acc_in, ml_in = refs.pop(0), refs.pop(0)
    if final:
        out_ref = refs.pop(0)
    else:
        acc_out, ml_out = refs.pop(0), refs.pop(0)
    kv_lo, kv_hi, qs, m_ref, l_ref, acc_ref, q_vmem, ml_vmem, sems = refs
    q_copy = pltpu.make_async_copy(q_ref, q_vmem, sems.at[0])
    q_copy.start()
    ctx = ctx_ref[0]
    z, x = ctx // NX, lax.rem(ctx, NX)
    b = pair_ref[ctx]

    places = [(ref, j, dz, dx) for ref, at in zip(srcs, blocks) for j, (dz, dx) in enumerate(at)]
    n = len(places)
    chunk = min(CHUNK, n * HALF)
    pairs = [pair_ref[lax.rem(z + NZ - dz, NZ) * NX + lax.rem(x + NX - dx, NX)] for _, _, dz, dx in places]
    ranks, low, high = [], [], []
    n_lo = n_hi = jnp.int32(0)
    for i, (ref, j, _, _) in enumerate(places):
        rank = jnp.int32(0)
        for k in range(n):
            if k != i:
                rank = rank + (pairs[k] < pairs[i]).astype(jnp.int32)
        n_lo = n_lo + (pairs[i] < b).astype(jnp.int32)
        n_hi = n_hi + (pairs[i] > b).astype(jnp.int32)
        ranks.append(rank)
        copy = pltpu.make_async_copy(
            ref.at[j, pl.ds(0, HALF)], kv_lo.at[pl.ds(pl.multiple_of(rank * HALF, HALF), HALF)], sems.at[4 + i]
        )
        copy.start()
        low.append(copy)
    for i, (ref, j, _, _) in enumerate(places):
        rank = n - 1 - ranks[i]
        copy = pltpu.make_async_copy(
            ref.at[j, pl.ds(HALF, HALF)], kv_hi.at[pl.ds(pl.multiple_of(rank * HALF, HALF), HALF)], sems.at[4 + n + i]
        )
        copy.start()
        high.append(copy)
    if not first:
        back = [
            pltpu.make_async_copy(acc_in, acc_ref, sems.at[1]),
            pltpu.make_async_copy(ml_in, ml_vmem, sems.at[2]),
        ]
        for copy in back:
            copy.start()
    q_copy.wait()
    for part in range(2):
        for kv in range(KV_LOC):
            rows = [
                q_vmem[part * HALF : (part + 1) * HALF, (kv * GROUP + g) * D : (kv * GROUP + g + 1) * D]
                for g in range(GROUP)
            ]
            t = jnp.transpose(jnp.concatenate(rows, axis=0).astype(jnp.float32) * C2)
            top = t.astype(jnp.bfloat16)
            qs[part, kv, :D, :] = top
            qs[part, kv, D:, :] = (t - top.astype(jnp.float32)).astype(jnp.bfloat16)
    if first:
        m_ref[...] = jnp.full_like(m_ref, NEG)
        l_ref[...] = jnp.zeros_like(l_ref)
        acc_ref[...] = jnp.zeros_like(acc_ref)
    else:
        for copy in back:
            copy.wait()
        m_ref[...] = ml_vmem[:, :, 0:1, :]
        l_ref[...] = ml_vmem[:, :, 1:2, :]
    if kv_lo.shape[0] > n * HALF:
        for ref in (kv_lo, kv_hi):
            ref[n * HALF :, :] = jnp.zeros((ref.shape[0] - n * HALF, ref.shape[1]), ref.dtype)
    for copy in low:
        copy.wait()

    def step(ref, part, start, limit, diag, width=chunk):
        keys, values = [], []
        for kv in range(KV_LOC):
            k = ref[pl.ds(start, width), kv * D : (kv + 1) * D]
            keys.append(jnp.concatenate([k, k], axis=1))
            values.append(ref[pl.ds(start, width), (KV_LOC + kv) * D : (KV_LOC + kv + 1) * D])

        def score(kv, r):
            s = dot(keys[kv], qs[part, kv, :, r : r + LANES])
            if limit is not None:
                pos = start + row_iota((width, LANES))
                own = limit + (lane_iota((width, LANES)) & (HALF - 1)) if diag else limit - 1
                s = jnp.where(pos <= own, s, NEG)
            return s

        def soft(kv, r, s):
            at = slice(r, r + LANES)
            old = m_ref[part, kv, :, at]
            new = jnp.maximum(old, jnp.max(s, axis=0, keepdims=True))
            alpha = jnp.exp2(old - new)
            p = jnp.exp2(s - new)
            m_ref[part, kv, :, at] = new
            l_ref[part, kv, :, at] = l_ref[part, kv, :, at] * alpha + jnp.sum(p, axis=0, keepdims=True)
            return alpha, p.astype(jnp.bfloat16)

        def mix(kv, r, alpha, p):
            at = slice(r, r + LANES)
            acc_ref[part, kv, :, at] = acc_ref[part, kv, :, at] * alpha + dot_tl(values[kv], p)

        units = [(kv, r) for kv in range(KV_LOC) for r in range(0, QROWS, LANES)]
        s = score(*units[0])
        pending = None
        for i, u in enumerate(units):
            following = score(*units[i + 1]) if i + 1 < len(units) else None
            if pending is not None:
                mix(*pending)
            pending = (*u, *soft(*u, s))
            s = following
        mix(*pending)

    def dense(ref, part, count):
        if isinstance(count, int):
            for i in range(count):
                step(ref, part, i * chunk, None, False)
            return

        @pl.loop(0, count)
        def _(i):
            step(ref, part, pl.multiple_of(i * chunk, chunk), None, False)

    def prefix(ref, part, count):
        limit = count * HALF
        full = limit // chunk
        dense(ref, part, full)
        start = pl.multiple_of(full * chunk, chunk)
        if first:
            step(ref, part, start, limit, True)
        else:

            @pl.when(limit > full * chunk)
            def _():
                step(ref, part, start, limit, False)

    dense(kv_lo, 1, n * HALF // chunk)
    if n * HALF % chunk:
        step(kv_lo, 1, n * HALF // chunk * chunk, None, False, n * HALF % chunk)
    prefix(kv_lo, 0, n_lo)
    for copy in high:
        copy.wait()
    prefix(kv_hi, 1, n_hi)
    if final:
        for part in range(2):
            for kv in range(KV_LOC):
                o = jnp.transpose(acc_ref[part, kv] / l_ref[part, kv])
                for g in range(GROUP):
                    h = kv * GROUP + g
                    out_ref[part * HALF : (part + 1) * HALF, h * D : (h + 1) * D] = o[g * HALF : (g + 1) * HALF].astype(
                        jnp.bfloat16
                    )
    else:
        acc_copy = pltpu.make_async_copy(acc_ref, acc_out, sems.at[1])
        acc_copy.start()
        ml_vmem[:, :, 0:1, :] = m_ref[...]
        ml_vmem[:, :, 1:2, :] = l_ref[...]
        ml_vmem[:, :, 2:, :] = jnp.zeros((2, KV_LOC, 6, QROWS), jnp.float32)
        ml_copy = pltpu.make_async_copy(ml_vmem, ml_out, sems.at[2])
        ml_copy.start()
        ml_copy.wait()
        acc_copy.wait()


def prefill(block_pair, ctx, queries, arrays, blocks, state, final):
    n = sum(len(at) for at in blocks)
    first = state is None
    chunk = min(CHUNK, n * HALF)
    rows = -(-n * HALF // chunk) * chunk
    acc = jax.ShapeDtypeStruct((2, KV_LOC, D, QROWS), jnp.float32)
    ml = jax.ShapeDtypeStruct((2, KV_LOC, 8, QROWS), jnp.float32)
    anywhere = pl.BlockSpec(memory_space=pl.ANY)
    return pl.pallas_call(
        functools.partial(prefill_kernel, blocks=blocks, first=first, final=final),
        out_shape=jax.ShapeDtypeStruct(queries.shape, jnp.bfloat16) if final else (acc, ml),
        in_specs=[pl.BlockSpec(memory_space=pltpu.SMEM)] * 2
        + [anywhere] * (1 + len(arrays) + (0 if first else 2)),
        out_specs=pl.BlockSpec(memory_space=pltpu.VMEM) if final else (anywhere, anywhere),
        scratch_shapes=[pltpu.VMEM((rows, 2 * KV_LOC * D), jnp.bfloat16)] * 2
        + [pltpu.VMEM((2, KV_LOC, 2 * D, QROWS), jnp.bfloat16)]
        + [pltpu.VMEM((2, KV_LOC, 1, QROWS), jnp.float32)] * 2
        + [
            pltpu.VMEM((2, KV_LOC, D, QROWS), jnp.float32),
            pltpu.VMEM(queries.shape, jnp.bfloat16),
            pltpu.VMEM((2, KV_LOC, 8, QROWS), jnp.float32),
            pltpu.SemaphoreType.DMA((4 + 2 * n,)),
        ],
        compiler_params=pltpu.CompilerParams(vmem_limit_bytes=VMEM_LIMIT),
        cost_estimate=pl.CostEstimate(
            flops=n * 2**28, bytes_accessed=4 * 2**20, transcendentals=n * 2**18
        ),
        name="prefill_end" if final else "prefill_start",
    )(block_pair, ctx, queries, *arrays, *(() if first else state))


def shift(x, dz, dx):
    def to(i):
        z, xx = divmod(i, NX)
        return ((z + dz) % NZ) * NX + (xx + dx) % NX

    return lax.ppermute(x, "ctx", [(i, to(i)) for i in range(N)])


def cat(*arrays):
    return jnp.concatenate(arrays, axis=0)


def join_kernel(*refs, ranges):
    *srcs, dst, sems = refs
    copies, at = [], 0
    for i, (src, (lo, hi)) in enumerate(zip(srcs, ranges)):
        copies.append(pltpu.make_async_copy(src.at[pl.ds(lo, hi - lo)], dst.at[pl.ds(at, hi - lo)], sems.at[i]))
        copies[-1].start()
        at += hi - lo
    for copy in copies:
        copy.wait()


def join(*pieces):
    arrays = [a for a, _, _ in pieces]
    ranges = [(lo, hi) for _, lo, hi in pieces]
    rows = sum(hi - lo for lo, hi in ranges)
    return pl.pallas_call(
        functools.partial(join_kernel, ranges=ranges),
        out_shape=jax.ShapeDtypeStruct((rows, *arrays[0].shape[1:]), arrays[0].dtype),
        in_specs=[pl.BlockSpec(memory_space=pl.ANY)] * len(arrays),
        out_specs=pl.BlockSpec(memory_space=pltpu.VMEM),
        scratch_shapes=[pltpu.SemaphoreType.DMA((len(arrays),))],
        cost_estimate=pl.CostEstimate(flops=0, bytes_accessed=rows * 2**18, transcendentals=0),
        name="join",
    )(*arrays)


def after(x, *others):
    return lax.optimization_barrier((x, *others))[0]


def local(
    prefill_queries,
    prefill_keys,
    prefill_values,
    block_pair,
    decode_queries,
    cache_keys,
    cache_values,
    draft_keys,
    draft_values,
    cache_len,
):
    ctx = lax.axis_index("ctx").astype(jnp.int32).reshape(1)
    pad = ((0, 0), (0, 8 - STEPS), (0, 0))
    dk8, dv8 = jnp.pad(draft_keys, pad), jnp.pad(draft_values, pad)

    own = jnp.concatenate([prefill_keys, prefill_values], axis=1)[None]
    up1, down1 = shift(own, 1, 0), shift(own, -1, 0)
    turned = jnp.transpose(decode_queries, (1, 0, 2))
    half = decode_partials(ctx, cache_len, turned, cache_keys, cache_values, None)
    near, near_z = cat(own, after(up1, *half), down1), [0, 1, -1]
    right1, left1, across1 = shift(near, 0, 1), shift(near, 0, -1), shift(near, 0, 2)
    up2, down2 = shift(near[:2], 2, 0), shift(cat(own, down1), -2, 0)

    partials, q72 = decode_partials(ctx, after(cache_len, up1, down1), turned, cache_keys, cache_values, half)

    up4 = shift(after(up2[1:], partials), 1, 0)
    recv = lax.all_to_all(after(partials, right1, left1, up2, down2, up4, across1), "ctx", 0, 0, tiled=True)
    far, far_z = join((up2, 0, 2), (down2, 0, 2), (up4, 0, 1)), [2, 3, -2, -3, 4]
    right2, left2 = shift(far, 0, 1), shift(far, 0, -1)

    def at(zs, x):
        return [(d, x) for d in zs]

    state = prefill(
        block_pair,
        ctx,
        prefill_queries,
        [near, right1, left1, across1, far],
        [at(near_z, 0), at(near_z, 1), at(near_z, -1), at(near_z, 2), at(far_z, 0)],
        None,
        False,
    )
    done = combine(after(ctx, *state, right2, left2), recv, q72, dk8, dv8)
    spread = lax.all_to_all(done, "ctx", 0, 0, tiled=True)
    decode_out = spread.reshape(REQ, STEPS, H_LOC * D)

    right3, left3 = shift(right2[:3], 0, 1), shift(left2[3:], 0, -1)
    state = prefill(
        after(block_pair, done), ctx, prefill_queries, [right2, left2], [at(far_z, 1), at(far_z, -1)], state, False
    )
    last = [at(far_z[:3], 2), at(far_z[3:], 2)]
    prefill_out = prefill(block_pair, ctx, prefill_queries, [right3, left3], last, state, True)
    return (prefill_out, decode_out)


def solution(mesh):
    return jax.shard_map(
        local,
        mesh=mesh,
        in_specs=(
            P(("rep", "ctx"), "head"),
            P(("rep", "ctx"), "head"),
            P(("rep", "ctx"), "head"),
            P("rep"),
            P("rep", None, "head"),
            P("rep", "ctx", "head"),
            P("rep", "ctx", "head"),
            P("rep", None, "head"),
            P("rep", None, "head"),
            P("rep"),
        ),
        out_specs=(P(("rep", "ctx"), "head"), P("rep", None, "head")),
        check_vma=False,
    )
```

```python
import functools

import jax
import jax.numpy as jnp
from jax import lax
from jax.experimental import pallas as pl
from jax.experimental.pallas import tpu as pltpu
from jax.sharding import PartitionSpec as P

D = 128
HEADS = 96
KV_HEADS = 8
GROUP = HEADS // KV_HEADS
KV_LOC = 2
H_LOC = KV_LOC * GROUP
HALF = 64
NZ, NX = 8, 4
N = NZ * NX
REQ = 32
STEPS = 3
ROWS = STEPS * H_LOC
PAY = ROWS + 8
NEG = -1e30
C2 = float(D**-0.5 * 1.4426950408889634)
CHUNK = 512
LANES = 256
QROWS = GROUP * HALF
VMEM_LIMIT = 60 * 1024 * 1024
RB = 8


def row_iota(shape):
    return lax.broadcasted_iota(jnp.int32, shape, 0)


def lane_iota(shape):
    return lax.broadcasted_iota(jnp.int32, shape, 1)


def dot_t(a, b):
    return lax.dot_general(a, b, (((1,), (1,)), ((), ())), preferred_element_type=jnp.float32)


def dot(a, b):
    return lax.dot_general(a, b, (((1,), (0,)), ((), ())), preferred_element_type=jnp.float32)


def dot_tl(a, b):
    return lax.dot_general(a, b, (((0,), (0,)), ((), ())), preferred_element_type=jnp.float32)


def to_lanes(col_bc, rows):
    diag = row_iota((rows, D)) == lane_iota((rows, D))
    return jnp.sum(jnp.where(diag, col_bc, 0.0), axis=0, keepdims=True)


def split(x, terms):
    out = []
    for _ in range(terms):
        out.append(x.astype(jnp.bfloat16).astype(jnp.float32))
        x = x - out[-1]
    return out


def decode_kernel(base, carried, ctx_ref, len_ref, q_ref, k_ref, v_ref, *refs):
    out_ref, q72_ref = refs[carried:]
    first = ctx_ref[0] * D
    step = base + pl.program_id(0)
    shape = (ROWS, 2 * D)
    lane = lane_iota(shape)
    kv_of_row = (lax.rem(row_iota(shape), H_LOC) >= GROUP).astype(jnp.int32)
    kv_of_lane = (lane >= D).astype(jnp.int32)
    same = kv_of_row == kv_of_lane
    slot = jnp.where(lane >= D, lane - D, lane) + first
    sub = row_iota((8, D))
    for t in range(STEPS):
        heads = [q_ref[t, :, h * D : (h + 1) * D].astype(jnp.float32) for h in range(H_LOC)]
        turned = jnp.transpose(jnp.stack(heads), (1, 0, 2))
        q72_ref[:, t * H_LOC : (t + 1) * H_LOC, :] = turned.astype(jnp.bfloat16)

    def score(i):
        k = k_ref[i]
        k2 = jnp.concatenate([k[:, :D], k[:, D:]], axis=0)
        return dot_t(q72_ref[i], k2) * C2

    def soft(i, s):
        live = same & (slot < len_ref[step * RB + i])
        s = jnp.where(live, s, NEG)
        top = jnp.max(s, axis=1, keepdims=True)
        p = jnp.where(live, jnp.exp2(s - top), 0.0)
        return top, jnp.sum(p, axis=1, keepdims=True), p.astype(jnp.bfloat16)

    def mix(i, top, total, p):
        v = v_ref[i]
        o = dot(p, jnp.concatenate([v[:, :D], v[:, D:]], axis=0))
        tail = jnp.zeros((8, D), jnp.float32)
        for j, term in enumerate(split(top, 3) + split(total, 2)):
            tail = jnp.where(sub == j, to_lanes(jnp.broadcast_to(term, (ROWS, D)), ROWS), tail)
        out_ref[i] = jnp.concatenate([o, tail], axis=0).astype(jnp.bfloat16)

    scores = [score(i) for i in range(RB)]
    weights = [soft(i, s) for i, s in enumerate(scores)]
    for i, w in enumerate(weights):
        mix(i, *w)


def decode_partials(ctx, cache_len, queries, cache_k, cache_v, before):
    steps = REQ // RB // 2
    base = 0 if before is None else steps
    before = () if before is None else before
    kernel = functools.partial(decode_kernel, base, len(before))
    return pl.pallas_call(
        kernel,
        out_shape=(
            jax.ShapeDtypeStruct((REQ, PAY, D), jnp.bfloat16),
            jax.ShapeDtypeStruct((REQ, ROWS, D), jnp.bfloat16),
        ),
        grid_spec=pltpu.PrefetchScalarGridSpec(
            num_scalar_prefetch=2,
            grid=(steps,),
            in_specs=[
                pl.BlockSpec((STEPS, RB, H_LOC * D), lambda i, c, n: (0, base + i, 0)),
                pl.BlockSpec((RB, D, 2 * D), lambda i, c, n: (base + i, 0, 0)),
                pl.BlockSpec((RB, D, 2 * D), lambda i, c, n: (base + i, 0, 0)),
            ]
            + [pl.BlockSpec(memory_space=pl.ANY)] * len(before),
            out_specs=(
                pl.BlockSpec((RB, PAY, D), lambda i, c, n: (base + i, 0, 0)),
                pl.BlockSpec((RB, ROWS, D), lambda i, c, n: (base + i, 0, 0)),
            ),
        ),
        input_output_aliases={5 + i: i for i in range(len(before))},
        compiler_params=pltpu.CompilerParams(vmem_limit_bytes=VMEM_LIMIT),
        cost_estimate=pl.CostEstimate(
            flops=REQ * ROWS * 256 * D * 2, bytes_accessed=3 * 2**20, transcendentals=REQ * ROWS * 128
        ),
        name="decode_partials",
    )(ctx, cache_len, queries, cache_k, cache_v, *before)


def combine_kernel(ctx_ref, recv_ref, q_ref, dk_ref, dv_ref, out_ref):
    dk = dk_ref[0].astype(jnp.float32)
    dv = dv_ref[0].astype(jnp.float32)
    k2 = jnp.concatenate([dk[:, :D], dk[:, D:]], axis=0).astype(jnp.bfloat16)
    v2 = jnp.concatenate([dv[:, :D], dv[:, D:]], axis=0).astype(jnp.bfloat16)
    s = dot_t(q_ref[0], k2) * C2
    shape = (ROWS, 16)
    row, lane = row_iota(shape), lane_iota(shape)
    kv_of_row = (lax.rem(row, H_LOC) >= GROUP).astype(jnp.int32)
    kv_of_lane = (lane >= 8).astype(jnp.int32)
    token = jnp.where(lane >= 8, lane - 8, lane)
    time = (row >= H_LOC).astype(jnp.int32) + (row >= 2 * H_LOC).astype(jnp.int32)
    seen = (kv_of_row == kv_of_lane) & (token <= time)
    s = jnp.where(seen, s, NEG)
    d_top = jnp.max(s, axis=1, keepdims=True)
    p = jnp.where(seen, jnp.exp2(s - d_top), 0.0)
    d_total = jnp.sum(p, axis=1, keepdims=True)
    d_out = dot(p.astype(jnp.bfloat16), v2)
    d_m = to_lanes(jnp.broadcast_to(d_top, (ROWS, D)), ROWS)
    d_l = to_lanes(jnp.broadcast_to(d_total, (ROWS, D)), ROWS)

    tails = recv_ref[:, ROWS:, :].astype(jnp.float32)
    m = (tails[:, 0, :] + tails[:, 1, :]) + tails[:, 2, :]
    total = tails[:, 3, :] + tails[:, 4, :]
    top = jnp.maximum(jnp.max(m, axis=0, keepdims=True), d_m)
    w = jnp.exp2(m - top)
    w_d = jnp.exp2(d_m - top)
    whole = jnp.sum(w * total, axis=0, keepdims=True) + w_d * d_l
    inv = 1.0 / jnp.where(whole > 0.0, whole, 1.0)
    w_all = jnp.concatenate([w * inv, jnp.broadcast_to(w_d * inv, (8, D)), jnp.zeros((D - N - 8, D), jnp.float32)], axis=0)
    w_cols = jnp.transpose(w_all)[:ROWS]
    acc = d_out * w_cols[:, N : N + 1]
    for src in range(N):
        acc = acc + recv_ref[src, :ROWS, :].astype(jnp.float32) * w_cols[:, src : src + 1]
    out = acc.astype(jnp.bfloat16)
    for dst in range(N):
        out_ref[dst] = out


def combine(ctx, recv, q72, dk8, dv8):
    return pl.pallas_call(
        combine_kernel,
        out_shape=jax.ShapeDtypeStruct((N, ROWS, D), jnp.bfloat16),
        grid_spec=pltpu.PrefetchScalarGridSpec(
            num_scalar_prefetch=1,
            grid=(1,),
            in_specs=[
                pl.BlockSpec((N, PAY, D), lambda i, c: (0, 0, 0)),
                pl.BlockSpec((1, ROWS, D), lambda i, c: (c[0], 0, 0)),
                pl.BlockSpec((1, 8, 2 * D), lambda i, c: (c[0], 0, 0)),
                pl.BlockSpec((1, 8, 2 * D), lambda i, c: (c[0], 0, 0)),
            ],
            out_specs=pl.BlockSpec((N, ROWS, D), lambda i, c: (0, 0, 0)),
        ),
        compiler_params=pltpu.CompilerParams(vmem_limit_bytes=8 * 1024 * 1024),
        cost_estimate=pl.CostEstimate(flops=4 * 2**20, bytes_accessed=2**20, transcendentals=2**14),
        name="combine",
    )(ctx, recv, q72, dk8, dv8)


def prefill_kernel(pair_ref, ctx_ref, *refs, blocks, first, final):
    refs = list(refs)
    q_ref = refs.pop(0)
    srcs = [refs.pop(0) for _ in blocks]
    if not first:
        acc_in, ml_in = refs.pop(0), refs.pop(0)
    if final:
        out_ref = refs.pop(0)
    else:
        acc_out, ml_out = refs.pop(0), refs.pop(0)
    kv_lo, kv_hi, qs, m_ref, l_ref, acc_ref, q_vmem, ml_vmem, sems = refs
    q_copy = pltpu.make_async_copy(q_ref, q_vmem, sems.at[0])
    q_copy.start()
    ctx = ctx_ref[0]
    z, x = ctx // NX, lax.rem(ctx, NX)
    b = pair_ref[ctx]

    places = [(ref, j, dz, dx) for ref, at in zip(srcs, blocks) for j, (dz, dx) in enumerate(at)]
    n = len(places)
    chunk = min(CHUNK, n * HALF)
    pairs = [pair_ref[lax.rem(z + NZ - dz, NZ) * NX + lax.rem(x + NX - dx, NX)] for _, _, dz, dx in places]
    ranks, low, high = [], [], []
    n_lo = n_hi = jnp.int32(0)
    for i, (ref, j, _, _) in enumerate(places):
        rank = jnp.int32(0)
        for k in range(n):
            if k != i:
                rank = rank + (pairs[k] < pairs[i]).astype(jnp.int32)
        n_lo = n_lo + (pairs[i] < b).astype(jnp.int32)
        n_hi = n_hi + (pairs[i] > b).astype(jnp.int32)
        ranks.append(rank)
        copy = pltpu.make_async_copy(
            ref.at[j, pl.ds(0, HALF)], kv_lo.at[pl.ds(pl.multiple_of(rank * HALF, HALF), HALF)], sems.at[4 + i]
        )
        copy.start()
        low.append(copy)
    for i, (ref, j, _, _) in enumerate(places):
        rank = n - 1 - ranks[i]
        copy = pltpu.make_async_copy(
            ref.at[j, pl.ds(HALF, HALF)], kv_hi.at[pl.ds(pl.multiple_of(rank * HALF, HALF), HALF)], sems.at[4 + n + i]
        )
        copy.start()
        high.append(copy)
    if not first:
        back = [
            pltpu.make_async_copy(acc_in, acc_ref, sems.at[1]),
            pltpu.make_async_copy(ml_in, ml_vmem, sems.at[2]),
        ]
        for copy in back:
            copy.start()
    q_copy.wait()
    for part in range(2):
        for kv in range(KV_LOC):
            rows = [
                q_vmem[part * HALF : (part + 1) * HALF, (kv * GROUP + g) * D : (kv * GROUP + g + 1) * D]
                for g in range(GROUP)
            ]
            t = jnp.transpose(jnp.concatenate(rows, axis=0).astype(jnp.float32) * C2)
            top = t.astype(jnp.bfloat16)
            qs[part, kv, :D, :] = top
            qs[part, kv, D:, :] = (t - top.astype(jnp.float32)).astype(jnp.bfloat16)
    if first:
        m_ref[...] = jnp.full_like(m_ref, NEG)
        l_ref[...] = jnp.zeros_like(l_ref)
        acc_ref[...] = jnp.zeros_like(acc_ref)
    else:
        for copy in back:
            copy.wait()
        m_ref[...] = ml_vmem[:, :, 0:1, :]
        l_ref[...] = ml_vmem[:, :, 1:2, :]
    if kv_lo.shape[0] > n * HALF:
        for ref in (kv_lo, kv_hi):
            ref[n * HALF :, :] = jnp.zeros((ref.shape[0] - n * HALF, ref.shape[1]), ref.dtype)
    for copy in low:
        copy.wait()

    def step(ref, part, start, limit, diag, width=chunk):
        keys, values = [], []
        for kv in range(KV_LOC):
            k = ref[pl.ds(start, width), kv * D : (kv + 1) * D]
            keys.append(jnp.concatenate([k, k], axis=1))
            values.append(ref[pl.ds(start, width), (KV_LOC + kv) * D : (KV_LOC + kv + 1) * D])

        def score(kv, r):
            s = dot(keys[kv], qs[part, kv, :, r : r + LANES])
            if limit is not None:
                pos = start + row_iota((width, LANES))
                own = limit + (lane_iota((width, LANES)) & (HALF - 1)) if diag else limit - 1
                s = jnp.where(pos <= own, s, NEG)
            return s

        def soft(kv, r, s):
            at = slice(r, r + LANES)
            old = m_ref[part, kv, :, at]
            new = jnp.maximum(old, jnp.max(s, axis=0, keepdims=True))
            alpha = jnp.exp2(old - new)
            p = jnp.exp2(s - new)
            m_ref[part, kv, :, at] = new
            l_ref[part, kv, :, at] = l_ref[part, kv, :, at] * alpha + jnp.sum(p, axis=0, keepdims=True)
            return alpha, p.astype(jnp.bfloat16)

        def mix(kv, r, alpha, p):
            at = slice(r, r + LANES)
            acc_ref[part, kv, :, at] = acc_ref[part, kv, :, at] * alpha + dot_tl(values[kv], p)

        units = [(kv, r) for kv in range(KV_LOC) for r in range(0, QROWS, LANES)]
        s = score(*units[0])
        pending = None
        for i, u in enumerate(units):
            following = score(*units[i + 1]) if i + 1 < len(units) else None
            if pending is not None:
                mix(*pending)
            pending = (*u, *soft(*u, s))
            s = following
        mix(*pending)

    def dense(ref, part, count):
        if isinstance(count, int):
            for i in range(count):
                step(ref, part, i * chunk, None, False)
            return

        @pl.loop(0, count)
        def _(i):
            step(ref, part, pl.multiple_of(i * chunk, chunk), None, False)

    def prefix(ref, part, count):
        limit = count * HALF
        full = limit // chunk
        dense(ref, part, full)
        start = pl.multiple_of(full * chunk, chunk)
        if first:
            step(ref, part, start, limit, True)
        else:

            @pl.when(limit > full * chunk)
            def _():
                step(ref, part, start, limit, False)

    dense(kv_lo, 1, n * HALF // chunk)
    if n * HALF % chunk:
        step(kv_lo, 1, n * HALF // chunk * chunk, None, False, n * HALF % chunk)
    prefix(kv_lo, 0, n_lo)
    for copy in high:
        copy.wait()
    prefix(kv_hi, 1, n_hi)
    if final:
        for part in range(2):
            for kv in range(KV_LOC):
                o = jnp.transpose(acc_ref[part, kv] / l_ref[part, kv])
                for g in range(GROUP):
                    h = kv * GROUP + g
                    out_ref[part * HALF : (part + 1) * HALF, h * D : (h + 1) * D] = o[g * HALF : (g + 1) * HALF].astype(
                        jnp.bfloat16
                    )
    else:
        acc_copy = pltpu.make_async_copy(acc_ref, acc_out, sems.at[1])
        acc_copy.start()
        ml_vmem[:, :, 0:1, :] = m_ref[...]
        ml_vmem[:, :, 1:2, :] = l_ref[...]
        ml_vmem[:, :, 2:, :] = jnp.zeros((2, KV_LOC, 6, QROWS), jnp.float32)
        ml_copy = pltpu.make_async_copy(ml_vmem, ml_out, sems.at[2])
        ml_copy.start()
        ml_copy.wait()
        acc_copy.wait()


def prefill(block_pair, ctx, queries, arrays, blocks, state, final):
    n = sum(len(at) for at in blocks)
    first = state is None
    chunk = min(CHUNK, n * HALF)
    rows = -(-n * HALF // chunk) * chunk
    acc = jax.ShapeDtypeStruct((2, KV_LOC, D, QROWS), jnp.float32)
    ml = jax.ShapeDtypeStruct((2, KV_LOC, 8, QROWS), jnp.float32)
    anywhere = pl.BlockSpec(memory_space=pl.ANY)
    return pl.pallas_call(
        functools.partial(prefill_kernel, blocks=blocks, first=first, final=final),
        out_shape=jax.ShapeDtypeStruct(queries.shape, jnp.bfloat16) if final else (acc, ml),
        in_specs=[pl.BlockSpec(memory_space=pltpu.SMEM)] * 2
        + [anywhere] * (1 + len(arrays) + (0 if first else 2)),
        out_specs=pl.BlockSpec(memory_space=pltpu.VMEM) if final else (anywhere, anywhere),
        scratch_shapes=[pltpu.VMEM((rows, 2 * KV_LOC * D), jnp.bfloat16)] * 2
        + [pltpu.VMEM((2, KV_LOC, 2 * D, QROWS), jnp.bfloat16)]
        + [pltpu.VMEM((2, KV_LOC, 1, QROWS), jnp.float32)] * 2
        + [
            pltpu.VMEM((2, KV_LOC, D, QROWS), jnp.float32),
            pltpu.VMEM(queries.shape, jnp.bfloat16),
            pltpu.VMEM((2, KV_LOC, 8, QROWS), jnp.float32),
            pltpu.SemaphoreType.DMA((4 + 2 * n,)),
        ],
        compiler_params=pltpu.CompilerParams(vmem_limit_bytes=VMEM_LIMIT),
        cost_estimate=pl.CostEstimate(
            flops=n * 2**28, bytes_accessed=4 * 2**20, transcendentals=n * 2**18
        ),
        name="prefill_end" if final else "prefill_start",
    )(block_pair, ctx, queries, *arrays, *(() if first else state))


def shift(x, dz, dx):
    def to(i):
        z, xx = divmod(i, NX)
        return ((z + dz) % NZ) * NX + (xx + dx) % NX

    return lax.ppermute(x, "ctx", [(i, to(i)) for i in range(N)])


def cat(*arrays):
    return jnp.concatenate(arrays, axis=0)


def join_kernel(*refs, ranges):
    *srcs, dst, sems = refs
    copies, at = [], 0
    for i, (src, (lo, hi)) in enumerate(zip(srcs, ranges)):
        copies.append(pltpu.make_async_copy(src.at[pl.ds(lo, hi - lo)], dst.at[pl.ds(at, hi - lo)], sems.at[i]))
        copies[-1].start()
        at += hi - lo
    for copy in copies:
        copy.wait()


def join(*pieces):
    arrays = [a for a, _, _ in pieces]
    ranges = [(lo, hi) for _, lo, hi in pieces]
    rows = sum(hi - lo for lo, hi in ranges)
    return pl.pallas_call(
        functools.partial(join_kernel, ranges=ranges),
        out_shape=jax.ShapeDtypeStruct((rows, *arrays[0].shape[1:]), arrays[0].dtype),
        in_specs=[pl.BlockSpec(memory_space=pl.ANY)] * len(arrays),
        out_specs=pl.BlockSpec(memory_space=pltpu.VMEM),
        scratch_shapes=[pltpu.SemaphoreType.DMA((len(arrays),))],
        cost_estimate=pl.CostEstimate(flops=0, bytes_accessed=rows * 2**18, transcendentals=0),
        name="join",
    )(*arrays)


def after(x, *others):
    return lax.optimization_barrier((x, *others))[0]


def local(
    prefill_queries,
    prefill_keys,
    prefill_values,
    block_pair,
    decode_queries,
    cache_keys,
    cache_values,
    draft_keys,
    draft_values,
    cache_len,
):
    ctx = lax.axis_index("ctx").astype(jnp.int32).reshape(1)
    pad = ((0, 0), (0, 8 - STEPS), (0, 0))
    dk8, dv8 = jnp.pad(draft_keys, pad), jnp.pad(draft_values, pad)

    own = jnp.concatenate([prefill_keys, prefill_values], axis=1)[None]
    up1, down1 = shift(own, 1, 0), shift(own, -1, 0)
    turned = jnp.transpose(decode_queries, (1, 0, 2))
    half = decode_partials(ctx, cache_len, turned, cache_keys, cache_values, None)
    near, near_z = cat(after(up1, *half), own, down1), [1, 0, -1]
    right1, left1, across1 = shift(near, 0, 1), shift(near, 0, -1), shift(near, 0, 2)
    up2, down2 = shift(near[:2], 2, 0), shift(near[1:], -2, 0)

    partials, q72 = decode_partials(ctx, after(cache_len, up1, down1), turned, cache_keys, cache_values, half)

    up4 = shift(after(up2[:1], partials), 1, 0)
    recv = lax.all_to_all(after(partials, right1, left1, up2, down2, up4, across1), "ctx", 0, 0, tiled=True)
    far, far_z = join((up2, 0, 2), (down2, 0, 2), (up4, 0, 1)), [3, 2, -2, -3, 4]
    right2, left2 = shift(far, 0, 1), shift(far, 0, -1)

    def at(zs, x):
        return [(d, x) for d in zs]

    state = prefill(
        block_pair,
        ctx,
        prefill_queries,
        [near, right1, left1, across1, far],
        [at(near_z, 0), at(near_z, 1), at(near_z, -1), at(near_z, 2), at(far_z, 0)],
        None,
        False,
    )
    done = combine(after(ctx, *state, right2, left2), recv, q72, dk8, dv8)
    spread = lax.all_to_all(done, "ctx", 0, 0, tiled=True)
    decode_out = spread.reshape(REQ, STEPS, H_LOC * D)

    right3, left3 = shift(right2[:3], 0, 1), shift(left2[3:], 0, -1)
    state = prefill(
        after(block_pair, done), ctx, prefill_queries, [right2, left2], [at(far_z, 1), at(far_z, -1)], state, False
    )
    last = [at(far_z[:3], 2), at(far_z[3:], 2)]
    prefill_out = prefill(block_pair, ctx, prefill_queries, [right3, left3], last, state, True)
    return (prefill_out, decode_out)


def solution(mesh):
    return jax.shard_map(
        local,
        mesh=mesh,
        in_specs=(
            P(("rep", "ctx"), "head"),
            P(("rep", "ctx"), "head"),
            P(("rep", "ctx"), "head"),
            P("rep"),
            P("rep", None, "head"),
            P("rep", "ctx", "head"),
            P("rep", "ctx", "head"),
            P("rep", None, "head"),
            P("rep", None, "head"),
            P("rep"),
        ),
        out_specs=(P(("rep", "ctx"), "head"), P("rep", None, "head")),
        check_vma=False,
    )
```
